128 devices in a mesh: occ: 16 (over x_lo, z, core), aux: 8 (over x_hi, y).
Axes of the slice: x: 4 (x_hi: 2, x_lo: 2; x = x_hi * 2 + x_lo), y: 4, z: 4, core: 2. Of those that a mesh axis runs over, the one named last changes fastest.
Arguments:
- orbital_b: bfloat16 [48, 256, 12288], P('occ', None, 'aux'), may hold values from -0.109375 to 0.109375
- block_size: int32 [16], replicated, may hold values from 1 to 3, 32 in all
- occ_energy: float32 [48], replicated, may hold values from -1.5 to -0.5
- virt_energy: float32 [256], replicated, may hold values from 0.2 to 1.2
Outputs:
- gamma: float32 [48, 256, 12288], P('occ', None, 'aux')
The draws below stay inside these ranges and needn't reach their ends.
Inputs may be any that keep to these rules, and one draw needn't show every extreme that they name: `block_size`: the sizes sum to 32; the largest is exactly 3.
All inputs are finite; a program needn't handle non-finite values.
Results may differ from the reference program's by a relative error of at most 0.0024.
Values may be sent and summed in bfloat16 or wider, within the bound.
A program may use at most 128 MiB of HBM per device.

```python
import math
import jax
import jax.numpy as jnp
import numpy as np
from jax import lax

SLOT = 3
VIRT = 256
STEPS = 4
AUX = 12288
OCC_ALL = 48
N_OCC = 16


def shard_levels(stream_key, extent, cuts, low, top_value):
    def one(dim, blocks):
        draws = jax.random.uniform(jax.random.fold_in(jax.random.fold_in(stream_key, 6), dim), (blocks,), jnp.float32, low / len(cuts), top_value / len(cuts))
        return jnp.repeat(jnp.exp(draws), extent[dim] // blocks).reshape((-1,) + (1,) * (len(extent) - dim - 1))

    loudness = one(*cuts[0])
    for cut in cuts[1:]:
        loudness = loudness * one(*cut)
    return loudness


def length_profile(amount, total, reach, skew):
    loads = [(1 << 20) // math.isqrt(standing ** skew) + 1 for standing in range(2, amount + 1)]
    rest, given = total - reach - (amount - 1), [1] * (amount - 1)
    while rest > 0:
        free = [i for i in range(amount - 1) if given[i] < reach]
        mass, budget = sum([loads[i] for i in free]), rest
        for i in free:
            more = min(reach - given[i], max(1, budget * loads[i] // mass), rest)
            given[i] = given[i] + more
            rest = rest - more
    return np.array([reach] + given)


def ragged_sizes(rng, number_of, total, reach, slope):
    if number_of == 2:
        one = jax.random.randint(rng, (), max(1, total - reach), min(reach, total - 1) + 1)
        return jnp.stack([one, total - one])
    sizes = jnp.asarray(length_profile(number_of, total, reach, slope), jnp.int32)
    pairs = (number_of - 1) // 2
    donor, receiver = sizes[1:1 + 2 * pairs:2], sizes[2:2 + 2 * pairs:2]
    slack = jnp.minimum(donor - 1, reach - receiver)
    shifted = jax.random.randint(jax.random.fold_in(rng, 1), (pairs,), 0, 1 << 20) % (slack + 1)
    sizes = sizes.at[1:1 + 2 * pairs:2].set(donor - shifted).at[2:2 + 2 * pairs:2].set(receiver + shifted)
    return sizes[jax.random.permutation(jax.random.fold_in(rng, 2), number_of)]


def scatter_about(own_key, extent, scale, limit, shards=(), kind=jnp.bfloat16):
    loudness = shard_levels(own_key, extent, shards, -0.22, 0.18) if shards else 1.0
    result = jax.random.normal(own_key, extent, jnp.float32) * scale * loudness
    return jnp.minimum(jnp.maximum(result, -limit), limit).astype(kind)


def setup_inputs(seed: int = 0) -> dict:
    key_list = jax.random.split(jax.random.key(seed), 5)
    orbital_b = scatter_about(key_list[0], (OCC_ALL, VIRT, AUX), (AUX // 4) ** -0.5, 0.109375, ((0, 16), (2, 8)))
    block_size = ragged_sizes(key_list[1], N_OCC, 2 * N_OCC, SLOT, 2).astype(jnp.int32)
    occ_energy = jnp.clip(jax.random.uniform(key_list[2], (OCC_ALL,), jnp.float32, -1.5, -0.5), -1.5, -0.5)
    virt_energy = jnp.clip(jax.random.uniform(key_list[3], (VIRT,), jnp.float32, 0.2, 1.2), 0.2, 1.2)
    return {"orbital_b": orbital_b, "block_size": block_size, "occ_energy": occ_energy, "virt_energy": virt_energy}


def reference(orbital_b, block_size, occ_energy, virt_energy):
    rows = jnp.arange(OCC_ALL, dtype=jnp.int32)
    owner = rows // SLOT
    valid = (rows % SLOT) < block_size[owner]
    live = jnp.where(valid[:, None, None], orbital_b, jnp.zeros_like(orbital_b))
    blocks = live.reshape(N_OCC, SLOT * VIRT, AUX)
    energies = occ_energy.reshape(N_OCC, SLOT)

    def row_energy(block):
        return (virt_energy[None, :] - energies[block][:, None]).reshape(SLOT * VIRT)

    def step(block, gamma):
        block = jnp.asarray(block).astype(jnp.int32)
        own = blocks[block]
        for offset in range(STEPS):
            other = ((block - offset) % N_OCC).astype(jnp.int32)
            slab = blocks[other]
            pair = lax.dot_general(own, slab, (((1,), (1,)), ((), ())), preferred_element_type=jnp.float32)
            denom = row_energy(block)[:, None] + row_energy(other)[None, :]
            amp = (pair / denom).astype(jnp.bfloat16)
            gamma = gamma.at[block].add(jnp.dot(amp, slab, preferred_element_type=jnp.float32))
            if offset > 0:
                back = lax.dot_general(amp, own, (((0,), (0,)), ((), ())), preferred_element_type=jnp.float32)
                gamma = gamma.at[other].add(back)
        return gamma

    gamma = lax.fori_loop(0, N_OCC, step, jnp.zeros((N_OCC, SLOT * VIRT, AUX), jnp.float32))
    return gamma.reshape(OCC_ALL, VIRT, AUX)
```

```python
import jax
import jax.numpy as jnp
from jax import lax
from jax.experimental import pallas as pl
from jax.experimental.pallas import tpu as pltpu
from jax.sharding import PartitionSpec as P

MESH = pl.DeviceIdType.MESH
BF16 = jnp.bfloat16
F32 = jnp.float32

SLAB_SHIFT = (0, 1, -1, -2, 2, 3)
PAIRS = ((0, 0), (1, 1), (1, 0), (0, 2), (1, 2), (4, 0), (4, 2), (1, 3))
N_PAIR = len(PAIRS)

STAGE_AT = dict(P=0.0, Q=2.5, R=5.5, T=10.0, U=14.0, V=17.0, W=20.0, Y=24.0, Z=27.0)
START = {0: 0.0, 2: 4.0, 1: 8.0, 5: 20.0, 3: 24.0, 6: 28.0, 4: 32.0, 7: 46.0}


def schedule():
    events = []
    for pair, begin in START.items():
        for stage, offset in STAGE_AT.items():
            events.append((begin + offset, stage, pair))
    for stage in "UVWYZ":
        events.append((START[7] + STAGE_AT[stage] + 3.0, stage, 8))
    return [(stage, pair) for _, stage, pair in sorted(events)]


def rows(start, size, align=16):
    return pl.ds(pl.multiple_of(start, align), size)


def kernel(orb, sizes, occ_e, virt, out, swap, slab, own, give, half, c1, d1, c2, e2, f2, amp,
           gam, bsend, brecv, vcol, s_swap, s_slab, s_half, s_c1, s_c2, s_f, s_ax, s_ay, s_fw,
           s_sib, s_z8, s_back, s_out):
    o = lax.axis_index("occ")
    a = lax.axis_index("aux")
    chip, core = o // 2, o % 2
    xh, y = a // 4, a % 4
    sibling = (chip * 2 + 1 - core, a)
    above = (((chip + 1) % 8) * 2 + core, a)
    below = (((chip + 7) % 8) * 2 + core, a)
    yup = (o, xh * 4 + (y + 1) % 4)
    ydn = (o, xh * 4 + (y + 3) % 4)
    xpart = (o, (1 - xh) * 4 + y)
    partners = (sibling, above, below, yup, ydn, xpart)

    barrier = pltpu.get_barrier_semaphore()
    for device in partners:
        pl.semaphore_signal(barrier, inc=1, device_id=device, device_id_type=MESH)
    pl.semaphore_wait(barrier, len(partners))

    pending = []

    def remote(src, dst, sems, device):
        copy = pltpu.make_async_remote_copy(
            src_ref=src, dst_ref=dst, send_sem=sems[0], recv_sem=sems[1], device_id=device,
            device_id_type=MESH)
        return copy

    def send(src, dst, sems, device):
        copy = remote(src, dst, sems, device)
        copy.start()
        pending.append(copy)
        return copy

    def landed(dst, sems):
        remote(dst, dst, sems, sibling).wait_recv()

    def pairsem(sem, *index):
        return sem.at[(0,) + index], sem.at[(1,) + index]

    mine = pl.ds(pl.multiple_of(core * 768, 128), 768)
    other = pl.ds(pl.multiple_of((1 - core) * 768, 128), 768)
    live = sizes[o]

    def mask_other(i, _):
        r = rows(i * 64, 64)
        swap[r, :] = jnp.where(i // 4 < live, orb[r, other], jnp.zeros((64, 768), BF16))
        return 0

    def mask_mine(i, _):
        r = rows(i * 64, 64)
        slab[core, r, :] = jnp.where(i // 4 < live, orb[r, mine], jnp.zeros((64, 768), BF16))
        return 0

    lax.fori_loop(0, 12, mask_other, 0)
    send(swap, slab.at[core], pairsem(s_swap), sibling)
    lax.fori_loop(0, 12, mask_mine, 0)

    column = jnp.broadcast_to(virt[...], (128, 256)).T
    vcol[0:256, :] = column
    vcol[256:512, :] = column

    landed(slab.at[1 - core], pairsem(s_swap))
    send(slab.at[1], slab.at[2], pairsem(s_slab, 0), above)
    send(slab.at[0], slab.at[4], pairsem(s_slab, 1), below)

    arrived = set()

    def need(index):
        if index < 2 or index in arrived:
            return
        if index in (2, 4):
            landed(slab.at[index], pairsem(s_slab, (index - 2) // 2))
            if index == 2:
                send(slab.at[0], slab.at[3], pairsem(s_slab, 2), above)
            else:
                send(slab.at[1], slab.at[5], pairsem(s_slab, 3), below)
        else:
            landed(slab.at[index], pairsem(s_slab, 2 + (index - 3) // 2))
        arrived.add(index)

    base = core * 384
    r_own = y * 96
    r_up = ((y + 1) % 4) * 96
    r_dn = ((y + 3) % 4) * 96
    r_far = ((y + 2) % 4) * 96
    gives = {}

    def stage_p(b):
        left, right = PAIRS[b]
        need(left)
        need(right)
        slot = b % 3
        if slot in gives:
            gives[slot].wait_send()

        def product(dst, first):
            def column_tile(n, _):
                dst[slot, :, pl.ds(pl.multiple_of(n * 256, 256), 256)] = lax.dot_general(
                    slab[left, rows(first, 384), :], slab[right, rows(n * 256, 256), :],
                    (((1,), (1,)), ((), ())), preferred_element_type=F32)
                return 0
            lax.fori_loop(0, 3, column_tile, 0)

        product(give, 384 - base)
        gives[slot] = remote(give.at[slot], half.at[b], pairsem(s_half, b), sibling)
        gives[slot].start()
        product(own, base)

    def stage_q(b):
        slot = b % 3
        landed(half.at[b], pairsem(s_half, b))

        def far(i, _):
            r = rows(r_far + i * 48, 48)
            c1[b, rows(i * 48, 48), :] = (half[b, r, :] + own[slot, r, :]).astype(BF16)
            return 0

        lax.fori_loop(0, 2, far, 0)
        send(c1.at[b, 0:48], d1.at[0, b], pairsem(s_c1, 0, b), yup)
        send(c1.at[b, 48:96], d1.at[1, b], pairsem(s_c1, 1, b), ydn)

        def add(i, _):
            r = rows(i * 48, 48)
            half[b, r, :] = half[b, r, :] + own[slot, r, :]
            return 0

        lax.fori_loop(0, 8, add, 0)

    def stage_r(b):
        landed(d1.at[0, b], pairsem(s_c1, 0, b))
        c2[0, b, 0:48, :] = (half[b, rows(r_up, 48), :] + d1[0, b].astype(F32)).astype(BF16)
        c2[0, b, 48:96, :] = half[b, rows(r_up + 48, 48), :].astype(BF16)
        send(c2.at[0, b], e2.at[0, b], pairsem(s_c2, 0, b), yup)
        landed(d1.at[1, b], pairsem(s_c1, 1, b))
        c2[1, b, 0:48, :] = half[b, rows(r_dn, 48), :].astype(BF16)
        c2[1, b, 48:96, :] = (half[b, rows(r_dn + 48, 48), :] + d1[1, b].astype(F32)).astype(BF16)
        send(c2.at[1, b], e2.at[1, b], pairsem(s_c2, 1, b), ydn)

    def stage_t(b):
        landed(e2.at[0, b], pairsem(s_c2, 0, b))
        landed(e2.at[1, b], pairsem(s_c2, 1, b))

        def total(i, _):
            r = rows(r_own + i * 48, 48)
            q = rows(i * 48, 48)
            half[b, r, :] = half[b, r, :] + (e2[0, b, q, :].astype(F32) + e2[1, b, q, :].astype(F32))
            return 0

        lax.fori_loop(0, 2, total, 0)
        send(half.at[b, rows(r_own + 48 * (1 - xh), 48)], f2.at[b], pairsem(s_f, b), xpart)

    def block(index):
        return (chip * 2 + SLAB_SHIFT[index] + 16) % 16

    def spot(yy, xx):
        return rows(base + ((yy + 4) % 4) * 96 + xx * 48, 48)

    def send_spot(b, where, sem, device):
        send(amp.at[b, where], amp.at[b, where], sem, device)

    def stage_u(b):
        here = spot(y, xh)
        if b < N_PAIR:
            landed(f2.at[b], pairsem(s_f, b))
            left, right = PAIRS[b]
            value = half[b, rows(r_own + 48 * xh, 48), :] + f2[b]
            first = base + r_own + 48 * xh
            within = first % 256
            e_row = block(left) * 3 + first // 256
            e_next = block(left) * 3 + jnp.minimum(first // 256 + 1, 2)
            step = lax.broadcasted_iota(jnp.int32, (48, 128), 0) + within
            row_e = vcol[rows(within, 48), :] - jnp.where(step < 256, occ_e[e_row], occ_e[e_next])
            row_e = jnp.concatenate([row_e, row_e], axis=1)
            for j in range(3):
                col_e = virt[...] - occ_e[block(right) * 3 + j]
                cols = slice(j * 256, j * 256 + 256)
                amp[b, here, cols] = (value[:, cols] / (row_e + col_e)).astype(BF16)
            if b == 7:
                send(amp.at[7, here], amp.at[8, here], pairsem(s_z8), below)
        else:
            landed(amp.at[8, here], pairsem(s_z8))
        send_spot(b, here, pairsem(s_ax, b), xpart)
        send_spot(b, here, pairsem(s_ay, 0, xh, b), yup)
        send_spot(b, here, pairsem(s_ay, 1, xh, b), ydn)

    def stage_v(b):
        there = spot(y, 1 - xh)
        landed(amp.at[b, there], pairsem(s_ax, b))
        send_spot(b, there, pairsem(s_ay, 0, 1 - xh, b), yup)
        send_spot(b, there, pairsem(s_ay, 1, 1 - xh, b), ydn)

    def stage_w(b):
        landed(amp.at[b, spot(y - 1, 0)], pairsem(s_ay, 0, 0, b))
        send_spot(b, spot(y - 1, 0), pairsem(s_fw, 0, b), yup)
        landed(amp.at[b, spot(y + 1, 1)], pairsem(s_ay, 1, 1, b))
        send_spot(b, spot(y + 1, 1), pairsem(s_fw, 1, b), ydn)

    def stage_y(b):
        landed(amp.at[b, spot(y - 1, 1)], pairsem(s_ay, 0, 1, b))
        landed(amp.at[b, spot(y + 1, 0)], pairsem(s_ay, 1, 0, b))
        landed(amp.at[b, spot(y + 2, 0)], pairsem(s_fw, 0, b))
        landed(amp.at[b, spot(y + 2, 1)], pairsem(s_fw, 1, b))
        part = rows(base, 384)
        send(amp.at[b, part], amp.at[b, part], pairsem(s_sib, b), sibling)

    def plain(b, s, k):
        return jnp.dot(amp[b, rows(k * 256, 256), :], slab[s], preferred_element_type=F32)

    def turned(b, s, k):
        return lax.dot_general(
            amp[b, :, pl.ds(pl.multiple_of(k * 256, 256), 256)], slab[s],
            (((0,), (0,)), ((), ())), preferred_element_type=F32)

    def accumulate(which, terms, first):
        def piece(k, _):
            r = rows(k * 256, 256)
            value = None if first else gam[which, r, :]
            for kind, b, s in terms:
                term = kind(b, s, k)
                value = term if value is None else value + term
            gam[which, r, :] = value
            return 0
        lax.fori_loop(0, 3, piece, 0)

    def hand_back(way, terms, device):
        for k in range(3):
            value = None
            for kind, b, s in terms:
                term = kind(b, s, k)
                value = term if value is None else value + term
            bsend[way, k * 256:(k + 1) * 256, :] = value.astype(BF16)
            part = slice(k * 256, (k + 1) * 256)
            send(bsend.at[way, part], brecv.at[way, part], pairsem(s_back, way, k), device)

    complete = set()

    def stage_z(b):
        away = rows(384 - base, 384)
        landed(amp.at[b, away], pairsem(s_sib, b))
        complete.add(b)
        if b == 6 or b == 5:
            if 5 in complete and 6 in complete:
                hand_back(0, [(plain, 5, 0), (plain, 6, 2)], above)
        if b in (3, 4, 6) and {3, 4, 6} <= complete:
            hand_back(1, [(turned, 3, 0), (turned, 4, 1), (turned, 6, 4)], below)
        if b < 3 and {0, 1, 2} <= complete:
            accumulate(0, [(plain, 0, 0), (turned, 2, 1)], True)
            accumulate(1, [(plain, 2, 0), (plain, 1, 1)], True)

    stages = dict(P=stage_p, Q=stage_q, R=stage_r, T=stage_t, U=stage_u, V=stage_v, W=stage_w,
                  Y=stage_y, Z=stage_z)
    for stage, b in schedule():
        stages[stage](b)
    need(5)
    accumulate(0, [(plain, 3, 2), (turned, 5, 4), (turned, 8, 5)], False)
    accumulate(1, [(plain, 4, 2), (plain, 7, 3)], False)

    locals_ = []
    for k in range(3):
        part = slice(k * 256, (k + 1) * 256)
        for way in range(2):
            landed(brecv.at[way, part], pairsem(s_back, way, k))
            gam[way, part, :] = gam[way, part, :] + brecv[way, part, :].astype(F32)
        send(gam.at[1 - core, part], out.at[part, mine], pairsem(s_out, k), sibling)
        copy = pltpu.make_async_copy(gam.at[core, part], out.at[part, mine], s_out.at[2, k])
        copy.start()
        locals_.append(copy)
    for k in range(3):
        landed(out.at[k * 256:(k + 1) * 256, other], pairsem(s_out, k))
    for copy in locals_:
        copy.wait()
    for copy in pending + list(gives.values()):
        copy.wait_send()


def per_device(orbital_b, block_size, occ_energy, virt_energy):
    block = orbital_b.reshape(768, 1536)
    dma = pltpu.SemaphoreType.DMA
    vmem = pltpu.VMEM
    result = pl.pallas_call(
        kernel,
        out_shape=jax.ShapeDtypeStruct((768, 1536), F32),
        in_specs=[
            pl.BlockSpec(memory_space=pltpu.VMEM),
            pl.BlockSpec(memory_space=pltpu.SMEM),
            pl.BlockSpec(memory_space=pltpu.SMEM),
            pl.BlockSpec(memory_space=pltpu.VMEM),
        ],
        out_specs=pl.BlockSpec(memory_space=pl.ANY),
        scratch_shapes=[
            vmem((768, 768), BF16),
            vmem((6, 768, 768), BF16),
            vmem((3, 384, 768), F32),
            vmem((3, 384, 768), F32),
            vmem((N_PAIR, 384, 768), F32),
            vmem((N_PAIR, 96, 768), BF16),
            vmem((2, N_PAIR, 48, 768), BF16),
            vmem((2, N_PAIR, 96, 768), BF16),
            vmem((2, N_PAIR, 96, 768), BF16),
            vmem((N_PAIR, 48, 768), F32),
            vmem((N_PAIR + 1, 768, 768), BF16),
            vmem((2, 768, 768), F32),
            vmem((2, 768, 768), BF16),
            vmem((2, 768, 768), BF16),
            vmem((512, 128), F32),
            dma((2,)),
            dma((2, 4)),
            dma((2, N_PAIR)),
            dma((2, 2, N_PAIR)),
            dma((2, 2, N_PAIR)),
            dma((2, N_PAIR)),
            dma((2, N_PAIR + 1)),
            dma((2, 2, 2, N_PAIR + 1)),
            dma((2, 2, N_PAIR + 1)),
            dma((2, N_PAIR + 1)),
            dma((2,)),
            dma((2, 2, 3)),
            dma((3, 3)),
        ],
        compiler_params=pltpu.CompilerParams(
            collective_id=0, has_side_effects=True, vmem_limit_bytes=62 * 2**20),
        name="window_gamma",
    )(block, block_size, occ_energy, virt_energy.reshape(1, 256))
    return result.reshape(3, 256, 1536)


def solution(mesh):
    in_specs = (P("occ", None, "aux"), P(), P(), P())
    out_specs = P("occ", None, "aux")
    return jax.shard_map(
        per_device, mesh=mesh, in_specs=in_specs, out_specs=out_specs, check_vma=False
    )
```

```python
import jax
import jax.numpy as jnp
from jax import lax
from jax.experimental import pallas as pl
from jax.experimental.pallas import tpu as pltpu
from jax.sharding import PartitionSpec as P

MESH = pl.DeviceIdType.MESH
BF16 = jnp.bfloat16
F32 = jnp.float32

SLAB_SHIFT = (0, 1, -1, -2, 2, 3)
BATCHES = (
    tuple((0, 0, k) for k in range(3)),
    tuple((1, 1, k) for k in range(3)),
    tuple((1, 0, k) for k in range(3)),
    ((0, 2, 0), (1, 2, 0), (0, 4, 0)),
    ((0, 2, 1), (1, 2, 1), (0, 4, 1)),
    ((0, 2, 2), (1, 2, 2), (0, 4, 2)),
    tuple((4, 2, k) for k in range(3)),
    tuple((1, 3, k) for k in range(3)),
)
N_PAIR = len(BATCHES)
AHEAD = 2

ORDER = (
    ("P", 2), ("P", 1), ("N", 0), ("Q", 2), ("Q", 1), ("P", 0), ("N", 1), ("R", 2), ("P", 3), ("N", 2),
    ("T", 2), ("Q", 3), ("R", 1), ("Q", 0), ("N", 3), ("R", 3), ("P", 4), ("N", 4), ("T", 1), ("Q", 4),
    ("R", 0), ("U", 2), ("N", 5), ("P", 6), ("N", 6), ("Q", 6), ("W", 2), ("T", 3), ("R", 6), ("Y", 2),
    ("N", 7), ("U", 1), ("Z", 2), ("R", 4), ("T", 6), ("N", 8), ("P", 5), ("W", 1), ("Q", 5), ("U", 3),
    ("N", 9), ("Y", 1), ("T", 4), ("Z", 1), ("T", 0), ("R", 5), ("U", 6), ("W", 3), ("T", 5), ("P", 7),
    ("W", 6), ("Q", 7), ("Y", 6), ("Y", 3), ("U", 4), ("R", 7), ("Z", 6), ("Z", 3), ("B", 0), ("W", 4),
    ("U", 0), ("U", 5), ("T", 7), ("Y", 4), ("Z", 4), ("B", 1), ("W", 0), ("W", 5), ("U", 7), ("Y", 0),
    ("Z", 0), ("Y", 5), ("A", 0), ("W", 7), ("U", 8), ("Y", 7), ("Z", 5), ("B", 2), ("Z", 7), ("W", 8),
    ("C", 0), ("Y", 8), ("Z", 8),
)


def rows(start, size, align=16):
    return pl.ds(pl.multiple_of(start, align), size)


def kernel(orb, sizes, occ_e, virt, out, back, swap, slab, own, give, half, c1, d1, c2, e2, f1, f2,
           amp, gam, bsend, vcol, s_swap, s_slab, s_half, s_c1, s_c2, s_f, s_ay, s_fw,
           s_sib, s_z8, s_back, s_out):
    o = lax.axis_index("occ")
    a = lax.axis_index("aux")
    chip, core = o // 2, o % 2
    xh, y = a // 4, a % 4
    sibling = (chip * 2 + 1 - core, a)
    up2 = ((chip + 1) % 8) * 2
    dn2 = ((chip + 7) % 8) * 2
    below = (dn2 + core, a)
    yup = (o, xh * 4 + (y + 1) % 4)
    ydn = (o, xh * 4 + (y + 3) % 4)
    xpart = (o, (1 - xh) * 4 + y)
    partners = (sibling, yup, ydn, xpart, (up2, a), (up2 + 1, a), (dn2, a), (dn2 + 1, a))

    barrier = pltpu.get_barrier_semaphore()
    for device in partners:
        pl.semaphore_signal(barrier, inc=1, device_id=device, device_id_type=MESH)
    pending = []

    def remote(src, dst, sems, device):
        copy = pltpu.make_async_remote_copy(
            src_ref=src, dst_ref=dst, send_sem=sems[0], recv_sem=sems[1], device_id=device,
            device_id_type=MESH)
        return copy

    def send(src, dst, sems, device):
        copy = remote(src, dst, sems, device)
        copy.start()
        pending.append(copy)
        return copy

    def landed(dst, sems):
        remote(dst, dst, sems, sibling).wait_recv()

    def pairsem(sem, *index):
        return sem.at[(0,) + index], sem.at[(1,) + index]

    mine = pl.ds(pl.multiple_of(core * 768, 128), 768)
    other = pl.ds(pl.multiple_of((1 - core) * 768, 128), 768)
    live = sizes[o]

    def mask_other(i, _):
        r = rows(i * 64, 64)
        swap[r, :] = jnp.where(i // 4 < live, orb[r, other], jnp.zeros((64, 768), BF16))
        return 0

    def mask_mine(i, _):
        r = rows(i * 64, 64)
        slab[core, r, :] = jnp.where(i // 4 < live, orb[r, mine], jnp.zeros((64, 768), BF16))
        return 0

    lax.fori_loop(0, 12, mask_other, 0)
    lax.fori_loop(0, 12, mask_mine, 0)
    pl.semaphore_wait(barrier, len(partners))

    def send_chunk(i):
        part = slice(i % 6 * 128, i % 6 * 128 + 128)
        for d, (which, index, chip2) in enumerate((
                (1 - i // 6, 2 + i // 6, up2), (i // 6, 4 + i // 6, dn2))):
            chunk = remote(slab.at[which, part], slab.at[index, part], pairsem(s_slab, d, i), (chip2 + core, a))
            chunk.start()
            chunks[d, i] = chunk

    chunks = {}
    send(swap.at[0:256], slab.at[core, 0:256], pairsem(s_swap, 0), sibling)
    send(swap.at[256:768], slab.at[core, 256:768], pairsem(s_swap, 1), sibling)
    landed(slab.at[1 - core, 0:256], pairsem(s_swap, 0))
    for i in range(AHEAD):
        send_chunk(i)

    column = jnp.broadcast_to(virt[...], (128, 256)).T
    vcol[0:256, :] = column
    vcol[256:512, :] = column

    landed(slab.at[1 - core, 256:768], pairsem(s_swap, 1))
    arrived = set()

    def need(index, k):
        if index < 2 or (index, k) in arrived:
            return
        d, late = (index - 2) // 2, index % 2 * 6
        for i in (2 * k, 2 * k + 1):
            landed(slab.at[index, i * 128:i * 128 + 128], pairsem(s_slab, d, late + i))
        arrived.add((index, k))

    def stage_n(i):
        for d in range(2):
            chunks[d, i].wait_send()
        send_chunk(i + AHEAD)

    base = core * 384
    r_own = y * 96
    r_up = ((y + 1) % 4) * 96
    r_dn = ((y + 3) % 4) * 96
    r_far = ((y + 2) % 4) * 96
    gives, taken = {}, {}

    def stage_p(b):
        for left, right, k in BATCHES[b]:
            need(right, k)
            for i in range(3):
                need(left, i)
        slot = taken[b] = min({0, 1, 2} - set(taken.values()))
        if slot in gives:
            gives[slot].wait_send()

        def product(dst, first):
            for j, (left, right, k) in enumerate(BATCHES[b]):
                dst[slot, :, j * 256:j * 256 + 256] = lax.dot_general(
                    slab[left, rows(first, 384), :], slab[right, k * 256:k * 256 + 256, :],
                    (((1,), (1,)), ((), ())), preferred_element_type=F32)

        product(give, 384 - base)
        gives[slot] = remote(give.at[slot], half.at[b], pairsem(s_half, b), sibling)
        gives[slot].start()
        product(own, base)

    def stage_q(b):
        slot = taken.pop(b)
        landed(half.at[b], pairsem(s_half, b))

        def far(i, _):
            r = rows(r_far + i * 48, 48)
            c1[b, rows(i * 48, 48), :] = (half[b, r, :] + own[slot, r, :]).astype(BF16)
            return 0

        lax.fori_loop(0, 2, far, 0)
        send(c1.at[b, 0:48], d1.at[0, b], pairsem(s_c1, 0, b), yup)
        send(c1.at[b, 48:96], d1.at[1, b], pairsem(s_c1, 1, b), ydn)

        def add(i, _):
            r = rows(i * 48, 48)
            half[b, r, :] = half[b, r, :] + own[slot, r, :]
            return 0

        lax.fori_loop(0, 8, add, 0)

    def stage_r(b):
        landed(d1.at[0, b], pairsem(s_c1, 0, b))
        c2[0, b, 0:48, :] = (half[b, rows(r_up, 48), :] + d1[0, b].astype(F32)).astype(BF16)
        c2[0, b, 48:96, :] = half[b, rows(r_up + 48, 48), :].astype(BF16)
        send(c2.at[0, b], e2.at[0, b], pairsem(s_c2, 0, b), yup)
        landed(d1.at[1, b], pairsem(s_c1, 1, b))
        c2[1, b, 0:48, :] = half[b, rows(r_dn, 48), :].astype(BF16)
        c2[1, b, 48:96, :] = (half[b, rows(r_dn + 48, 48), :] + d1[1, b].astype(F32)).astype(BF16)
        send(c2.at[1, b], e2.at[1, b], pairsem(s_c2, 1, b), ydn)

    def stage_t(b):
        landed(e2.at[0, b], pairsem(s_c2, 0, b))
        landed(e2.at[1, b], pairsem(s_c2, 1, b))

        def total(i, _):
            r = rows(r_own + i * 48, 48)
            q = rows(i * 48, 48)
            value = half[b, r, :] + (e2[0, b, q, :].astype(F32) + e2[1, b, q, :].astype(F32))
            half[b, r, :] = value
            f1[b, q, :] = value.astype(BF16)
            return 0

        lax.fori_loop(0, 2, total, 0)
        send(f1.at[b], f2.at[b], pairsem(s_f, b), xpart)

    def block(index):
        return (chip * 2 + SLAB_SHIFT[index] + 16) % 16

    def spot(yy):
        return rows(base + ((yy + 4) % 4) * 96, 96)

    def halfspot(yy, i):
        return rows(base + ((yy + 4) % 4) * 96 + i * 48, 48)

    def send_spot(b, where, sem, device):
        send(amp.at[b, where], amp.at[b, where], sem, device)

    def stage_u(b):
        here = spot(y)
        if b < N_PAIR:
            landed(f2.at[b], pairsem(s_f, b))
            first = base + r_own
            within = first % 256
            step = lax.broadcasted_iota(jnp.int32, (96, 128), 0) + within
            for j, (left, right, k) in enumerate(BATCHES[b]):
                e_row = block(left) * 3 + first // 256
                e_next = block(left) * 3 + jnp.minimum(first // 256 + 1, 2)
                row_e = vcol[rows(within, 96), :] - jnp.where(step < 256, occ_e[e_row], occ_e[e_next])
                row_e = jnp.concatenate([row_e, row_e], axis=1)
                col_e = virt[...] - occ_e[block(right) * 3 + k]
                lanes = slice(j * 256, j * 256 + 256)
                value = half[b, rows(r_own, 96), lanes] + f2[b, :, lanes].astype(F32)
                amp[b, here, lanes] = (value / (row_e + col_e)).astype(BF16)
            if b == 7:
                send(amp.at[7, here], amp.at[8, here], pairsem(s_z8), below)
        else:
            landed(amp.at[8, here], pairsem(s_z8))
        send_spot(b, here, pairsem(s_ay, 0, b), yup)
        send_spot(b, here, pairsem(s_ay, 1, b), ydn)

    def stage_w(b):
        landed(amp.at[b, spot(y - 1)], pairsem(s_ay, 0, b))
        send_spot(b, halfspot(y - 1, 0), pairsem(s_fw, 0, b), yup)
        landed(amp.at[b, spot(y + 1)], pairsem(s_ay, 1, b))
        send_spot(b, halfspot(y + 1, 1), pairsem(s_fw, 1, b), ydn)

    def stage_y(b):
        landed(amp.at[b, halfspot(y + 2, 0)], pairsem(s_fw, 0, b))
        landed(amp.at[b, halfspot(y + 2, 1)], pairsem(s_fw, 1, b))
        part = rows(base, 384)
        send(amp.at[b, part], amp.at[b, part], pairsem(s_sib, b), sibling)

    def cols(k):
        return slice(k * 256, k * 256 + 256)

    def plain(b, s):
        return lambda k: jnp.dot(amp[b, cols(k), :], slab[s], preferred_element_type=F32)

    def turned(b, s):
        return lambda k: lax.dot_general(
            amp[b, :, cols(k)], slab[s], (((0,), (0,)), ((), ())), preferred_element_type=F32)

    def turned_unit(j, s):
        return lambda k: lax.dot_general(
            amp[3 + k, :, cols(j)], slab[s], (((0,), (0,)), ((), ())), preferred_element_type=F32)

    def units(j, s):
        def term(k):
            value = None
            for i in range(3):
                part = jnp.dot(amp[3 + i, cols(k), cols(j)], slab[s, cols(i), :], preferred_element_type=F32)
                value = part if value is None else value + part
            return value
        return term

    def total_of(terms, k):
        value = terms[0](k)
        for term in terms[1:]:
            value = value + term(k)
        return value

    def accumulate(which, terms, first):
        for k in range(3):
            value = total_of(terms, k)
            gam[which, cols(k), :] = value if first else gam[which, cols(k), :] + value

    def hand_back(k):
        bsend[0, cols(k), :] = total_of(
            [turned_unit(0, 0), turned_unit(1, 1), turned(6, 4)], k).astype(BF16)
        send(bsend.at[0, cols(k)], back.at[cols(k), mine],
             (s_back.at[0, 0, k], s_back.at[1, core, k]), (dn2 + 1, a))
        bsend[1, cols(k), :] = total_of([turned_unit(2, 0), plain(6, 2)], k).astype(BF16)
        send(bsend.at[1, cols(k)], back.at[cols(k), mine],
             (s_back.at[0, 1, k], s_back.at[1, core, k]), (up2, a))

    def stage_z(b):
        landed(amp.at[b, rows(384 - base, 384)], pairsem(s_sib, b))

    def stage_a(_):
        accumulate(0, [plain(0, 0), turned(2, 1)], True)
        accumulate(1, [plain(2, 0), plain(1, 1)], True)

    def stage_c(_):
        accumulate(0, [units(0, 2), units(2, 4)], False)
        accumulate(1, [units(1, 2)], False)

    stages = dict(P=stage_p, Q=stage_q, R=stage_r, T=stage_t, U=stage_u, W=stage_w, Y=stage_y, Z=stage_z,
                  N=stage_n, B=hand_back, A=stage_a, C=stage_c)
    for stage, b in ORDER:
        stages[stage](b)
    for k in range(3):
        need(5, k)
    locals_ = []
    for k in range(3):
        for which, terms in ((0, [turned(8, 5)]), (1, [plain(7, 3)])):
            gam[which, cols(k), :] = gam[which, cols(k), :] + total_of(terms, k)
        send(gam.at[1 - core, cols(k)], out.at[cols(k), mine], pairsem(s_out, k), sibling)
        copy = pltpu.make_async_copy(gam.at[core, cols(k)], out.at[cols(k), mine], s_out.at[2, k])
        copy.start()
        locals_.append(copy)
    for k in range(3):
        landed(out.at[cols(k), other], pairsem(s_out, k))
        for j in range(2):
            landed(back.at[cols(k), j * 768:j * 768 + 768], (s_back.at[0, 0, k], s_back.at[1, j, k]))
    for copy in locals_:
        copy.wait()
    for i in range(12 - AHEAD, 12):
        for d in range(2):
            chunks[d, i].wait_send()
    for copy in pending + list(gives.values()):
        copy.wait_send()


def per_device(orbital_b, block_size, occ_energy, virt_energy):
    block = orbital_b.reshape(768, 1536)
    dma = pltpu.SemaphoreType.DMA
    vmem = pltpu.VMEM
    partial, shares = pl.pallas_call(
        kernel,
        out_shape=(jax.ShapeDtypeStruct((768, 1536), F32), jax.ShapeDtypeStruct((768, 1536), BF16)),
        in_specs=[
            pl.BlockSpec(memory_space=pltpu.VMEM),
            pl.BlockSpec(memory_space=pltpu.SMEM),
            pl.BlockSpec(memory_space=pltpu.SMEM),
            pl.BlockSpec(memory_space=pltpu.VMEM),
        ],
        out_specs=(pl.BlockSpec(memory_space=pl.ANY), pl.BlockSpec(memory_space=pl.ANY)),
        scratch_shapes=[
            vmem((768, 768), BF16),
            vmem((6, 768, 768), BF16),
            vmem((3, 384, 768), F32),
            vmem((3, 384, 768), F32),
            vmem((N_PAIR, 384, 768), F32),
            vmem((N_PAIR, 96, 768), BF16),
            vmem((2, N_PAIR, 48, 768), BF16),
            vmem((2, N_PAIR, 96, 768), BF16),
            vmem((2, N_PAIR, 96, 768), BF16),
            vmem((N_PAIR, 96, 768), BF16),
            vmem((N_PAIR, 96, 768), BF16),
            vmem((N_PAIR + 1, 768, 768), BF16),
            vmem((2, 768, 768), F32),
            vmem((2, 768, 768), BF16),
            vmem((512, 128), F32),
            dma((2, 2)),
            dma((2, 2, 12)),
            dma((2, N_PAIR)),
            dma((2, 2, N_PAIR)),
            dma((2, 2, N_PAIR)),
            dma((2, N_PAIR)),
            dma((2, 2, N_PAIR + 1)),
            dma((2, 2, N_PAIR + 1)),
            dma((2, N_PAIR + 1)),
            dma((2,)),
            dma((2, 2, 3)),
            dma((3, 3)),
        ],
        compiler_params=pltpu.CompilerParams(
            collective_id=0, has_side_effects=True, vmem_limit_bytes=62 * 2**20),
        name="window_gamma",
    )(block, block_size, occ_energy, virt_energy.reshape(1, 256))
    return (partial + shares.astype(F32)).reshape(3, 256, 1536)


def solution(mesh):
    in_specs = (P("occ", None, "aux"), P(), P(), P())
    out_specs = P("occ", None, "aux")
    return jax.shard_map(
        per_device, mesh=mesh, in_specs=in_specs, out_specs=out_specs, check_vma=False
    )
```

```python
import jax
import jax.numpy as jnp
from jax import lax
from jax.experimental import pallas as pl
from jax.experimental.pallas import tpu as pltpu
from jax.sharding import PartitionSpec as P

MESH = pl.DeviceIdType.MESH
BF16 = jnp.bfloat16
F32 = jnp.float32

SLAB_SHIFT = (0, 1, -1, -2, 2, 3)
PACKED = 3
BATCHES = (
    ((0, 0, 0), (0, 0, PACKED)),
    ((1, 1, 0), (1, 1, PACKED)),
    tuple((1, 0, k) for k in range(3)),
    ((0, 2, 0), (1, 2, 0), (0, 4, 0)),
    ((0, 2, 1), (1, 2, 1), (0, 4, 1)),
    ((0, 2, 2), (1, 2, 2), (0, 4, 2)),
    tuple((4, 2, k) for k in range(3)),
    tuple((1, 3, k) for k in range(3)),
)
N_PAIR = len(BATCHES)
AHEAD = 2

ORDER = (
    ("P", 0), ("P", 2), ("P", 1), ("Q", 0), ("Q", 2), ("N", 0), ("Q", 1), ("R", 2), ("N", 1), ("P", 3),
    ("N", 2), ("Q", 3), ("R", 3), ("R", 0), ("N", 3), ("P", 4), ("N", 4), ("T", 3), ("Q", 4), ("R", 1),
    ("R", 4), ("N", 5), ("T", 0), ("P", 5), ("P", 6), ("N", 6), ("Q", 6), ("R", 6), ("U", 3), ("N", 7),
    ("Q", 5), ("U", 0), ("T", 6), ("N", 8), ("W", 3), ("R", 5), ("T", 2), ("N", 9), ("W", 0), ("Y", 3),
    ("Z", 3), ("U", 6), ("T", 5), ("T", 4), ("T", 1), ("Y", 0), ("Z", 0), ("W", 6), ("U", 2), ("P", 7),
    ("Y", 6), ("Q", 7), ("Z", 6), ("U", 5), ("B", 0), ("R", 7), ("U", 4), ("U", 1), ("W", 5), ("T", 7),
    ("W", 4), ("W", 2), ("W", 1), ("Y", 5), ("U", 7), ("Z", 5), ("Y", 4), ("B", 2), ("Y", 2), ("Z", 4),
    ("B", 1), ("Y", 1), ("Z", 2), ("U", 8), ("W", 7), ("Z", 1), ("A", 1), ("A", 0), ("W", 8), ("C", 0),
    ("Y", 7), ("C", 1), ("Y", 8), ("Z", 7), ("D", 7), ("Z", 8), ("D", 8),
)


def rows(start, size, align=16):
    return pl.ds(pl.multiple_of(start, align), size)


def kernel(orb_hbm, sizes, occ_e, virt, out, back, orb, swap, slab, own, give, half, c1, d1, c2, e2, f1, f2,
           amp, gam, bsend, vcol, s_swap, s_slab, s_half, s_c1, s_c2, s_f, s_ay, s_fw,
           s_sib, s_z8, s_back, s_out, s_load):
    o = lax.axis_index("occ")
    a = lax.axis_index("aux")
    chip, core = o // 2, o % 2
    xh, y = a // 4, a % 4
    sibling = (chip * 2 + 1 - core, a)
    up2 = ((chip + 1) % 8) * 2
    dn2 = ((chip + 7) % 8) * 2
    below = (dn2 + core, a)
    yup = (o, xh * 4 + (y + 1) % 4)
    ydn = (o, xh * 4 + (y + 3) % 4)
    xpart = (o, (1 - xh) * 4 + y)
    partners = (sibling, yup, ydn, xpart, (up2, a), (up2 + 1, a), (dn2, a), (dn2 + 1, a))

    load = pltpu.make_async_copy(orb_hbm, orb, s_load)
    load.start()
    barrier = pltpu.get_barrier_semaphore()
    for device in partners:
        pl.semaphore_signal(barrier, inc=1, device_id=device, device_id_type=MESH)
    pending = []

    def remote(src, dst, sems, device):
        copy = pltpu.make_async_remote_copy(
            src_ref=src, dst_ref=dst, send_sem=sems[0], recv_sem=sems[1], device_id=device,
            device_id_type=MESH)
        return copy

    def send(src, dst, sems, device):
        copy = remote(src, dst, sems, device)
        copy.start()
        pending.append(copy)
        return copy

    def landed(dst, sems):
        remote(dst, dst, sems, sibling).wait_recv()

    def pairsem(sem, *index):
        return sem.at[(0,) + index], sem.at[(1,) + index]

    mine = pl.ds(pl.multiple_of(core * 768, 128), 768)
    other = pl.ds(pl.multiple_of((1 - core) * 768, 128), 768)
    live = sizes[o]

    def mask_other(i, _):
        r = rows(i * 64, 64)
        swap[r, :] = jnp.where(i // 4 < live, orb[r, other], jnp.zeros((64, 768), BF16))
        return 0

    def mask_mine(i, _):
        r = rows(i * 64, 64)
        slab[core, r, :] = jnp.where(i // 4 < live, orb[r, mine], jnp.zeros((64, 768), BF16))
        return 0

    load.wait()
    lax.fori_loop(0, 12, mask_other, 0)
    lax.fori_loop(0, 12, mask_mine, 0)
    pl.semaphore_wait(barrier, len(partners))

    def send_chunk(i):
        part = slice(i % 6 * 128, i % 6 * 128 + 128)
        for d, (which, index, chip2) in enumerate((
                (1 - i // 6, 2 + i // 6, up2), (i // 6, 4 + i // 6, dn2))):
            chunk = remote(slab.at[which, part], slab.at[index, part], pairsem(s_slab, d, i), (chip2 + core, a))
            chunk.start()
            chunks[d, i] = chunk

    chunks = {}
    send(swap.at[0:256], slab.at[core, 0:256], pairsem(s_swap, 0), sibling)
    send(swap.at[256:768], slab.at[core, 256:768], pairsem(s_swap, 1), sibling)
    landed(slab.at[1 - core, 0:256], pairsem(s_swap, 0))
    for i in range(AHEAD):
        send_chunk(i)

    column = jnp.broadcast_to(virt[...], (128, 256)).T
    vcol[0:256, :] = column
    vcol[256:512, :] = column

    landed(slab.at[1 - core, 256:768], pairsem(s_swap, 1))
    arrived = set()

    def need(index, k):
        if index < 2 or (index, k) in arrived:
            return
        d, late = (index - 2) // 2, index % 2 * 6
        for i in (2 * k, 2 * k + 1):
            landed(slab.at[index, i * 128:i * 128 + 128], pairsem(s_slab, d, late + i))
        arrived.add((index, k))

    def stage_n(i):
        for d in range(2):
            chunks[d, i].wait_send()
        send_chunk(i + AHEAD)

    base = core * 384
    r_own = y * 96
    r_up = ((y + 1) % 4) * 96
    r_dn = ((y + 3) % 4) * 96
    r_far = ((y + 2) % 4) * 96
    gives, taken = {}, {}

    def stage_p(b):
        for left, right, k in BATCHES[b]:
            need(right, k)
            for i in range(3):
                need(left, i)
        slot = taken[b] = min({0, 1, 2} - set(taken.values()))
        if slot in gives:
            gives[slot].wait_send()

        def product(dst, side):
            for j, (left, right, k) in enumerate(BATCHES[b]):
                lanes = slice(j * 256, j * 256 + 256)
                if k == PACKED:
                    for p in range(3):
                        row = 256 + 128 * p + side * (384, 128, 128)[p]
                        col = 256 + side * (0, 256, 256)[p]
                        dst[slot, p * 128:p * 128 + 128, lanes] = lax.dot_general(
                            slab[left, rows(row, 128), :], slab[right, rows(col, 256), :],
                            (((1,), (1,)), ((), ())), preferred_element_type=F32)
                else:
                    dst[slot, :, lanes] = lax.dot_general(
                        slab[left, rows(side * 384, 384), :], slab[right, k * 256:k * 256 + 256, :],
                        (((1,), (1,)), ((), ())), preferred_element_type=F32)

        w = wide(b)
        product(give, 1 - core)
        gives[slot] = remote(give.at[slot, :, w], half.at[b, :, w], pairsem(s_half, b), sibling)
        gives[slot].start()
        product(own, core)

    def wide(b):
        return slice(0, 256 * len(BATCHES[min(b, 7)]))

    def stage_q(b):
        slot, w = taken.pop(b), wide(b)
        landed(half.at[b, :, w], pairsem(s_half, b))

        def far(i, _):
            r = rows(r_far + i * 48, 48)
            c1[b, rows(i * 48, 48), w] = (half[b, r, w] + own[slot, r, w]).astype(BF16)
            return 0

        lax.fori_loop(0, 2, far, 0)
        send(c1.at[b, 0:48, w], d1.at[0, b, :, w], pairsem(s_c1, 0, b), yup)
        send(c1.at[b, 48:96, w], d1.at[1, b, :, w], pairsem(s_c1, 1, b), ydn)

        def add(i, _):
            r = rows(i * 48, 48)
            half[b, r, w] = half[b, r, w] + own[slot, r, w]
            return 0

        lax.fori_loop(0, 8, add, 0)

    def stage_r(b):
        w = wide(b)
        landed(d1.at[0, b, :, w], pairsem(s_c1, 0, b))
        c2[0, b, 0:48, w] = (half[b, rows(r_up, 48), w] + d1[0, b, :, w].astype(F32)).astype(BF16)
        c2[0, b, 48:96, w] = half[b, rows(r_up + 48, 48), w].astype(BF16)
        send(c2.at[0, b, :, w], e2.at[0, b, :, w], pairsem(s_c2, 0, b), yup)
        landed(d1.at[1, b, :, w], pairsem(s_c1, 1, b))
        c2[1, b, 0:48, w] = half[b, rows(r_dn, 48), w].astype(BF16)
        c2[1, b, 48:96, w] = (half[b, rows(r_dn + 48, 48), w] + d1[1, b, :, w].astype(F32)).astype(BF16)
        send(c2.at[1, b, :, w], e2.at[1, b, :, w], pairsem(s_c2, 1, b), ydn)

    def stage_t(b):
        w = wide(b)
        landed(e2.at[0, b, :, w], pairsem(s_c2, 0, b))
        landed(e2.at[1, b, :, w], pairsem(s_c2, 1, b))

        def total(i, _):
            r = rows(r_own + i * 48, 48)
            q = rows(i * 48, 48)
            value = half[b, r, w] + (e2[0, b, q, w].astype(F32) + e2[1, b, q, w].astype(F32))
            half[b, r, w] = value
            f1[b, q, w] = value.astype(BF16)
            return 0

        lax.fori_loop(0, 2, total, 0)
        send(f1.at[b, :, w], f2.at[b, :, w], pairsem(s_f, b), xpart)

    def block(index):
        return (chip * 2 + SLAB_SHIFT[index] + 16) % 16

    def spot(yy):
        return rows(base + ((yy + 4) % 4) * 96, 96)

    def halfspot(yy, i):
        return rows(base + ((yy + 4) % 4) * 96 + i * 48, 48)

    def send_spot(b, where, sem, device):
        send(amp.at[b, where, wide(b)], amp.at[b, where, wide(b)], sem, device)

    def stage_u(b):
        here = spot(y)
        if b < N_PAIR:
            landed(f2.at[b, :, wide(b)], pairsem(s_f, b))
            first = base + r_own
            within = first % 256
            group = first // 256
            after = jnp.minimum(group + 1, 2)
            step = lax.broadcasted_iota(jnp.int32, (96, 256), 0) + within
            down = vcol[rows(within, 96), :]
            down = jnp.concatenate([down, down], axis=1)
            for j, (left, right, k) in enumerate(BATCHES[b]):
                def energy(which, slots):
                    first_e = occ_e[block(which) * 3 + slots[0]]
                    return jnp.where(step < 256, first_e, occ_e[block(which) * 3 + slots[1]])
                if k == PACKED:
                    row_e = down - energy(left, (jnp.minimum(group + 1, 2), jnp.minimum(after + 1, 2)))
                    col_e = virt[...] - energy(right, (1 + group // 2, 1 + after // 2))
                else:
                    row_e = down - energy(left, (group, after))
                    col_e = virt[...] - occ_e[block(right) * 3 + k]
                lanes = slice(j * 256, j * 256 + 256)
                value = half[b, rows(r_own, 96), lanes] + f2[b, :, lanes].astype(F32)
                amp[b, here, lanes] = (value / (row_e + col_e)).astype(BF16)
            if b == 7:
                send(amp.at[7, here], amp.at[8, here], pairsem(s_z8), below)
        else:
            landed(amp.at[8, here], pairsem(s_z8))
        send_spot(b, here, pairsem(s_ay, 0, b), yup)
        send_spot(b, here, pairsem(s_ay, 1, b), ydn)

    def stage_w(b):
        w = wide(b)
        landed(amp.at[b, spot(y - 1), w], pairsem(s_ay, 0, b))
        send_spot(b, halfspot(y - 1, 0), pairsem(s_fw, 0, b), yup)
        landed(amp.at[b, spot(y + 1), w], pairsem(s_ay, 1, b))
        send_spot(b, halfspot(y + 1, 1), pairsem(s_fw, 1, b), ydn)

    def stage_y(b):
        w = wide(b)
        landed(amp.at[b, halfspot(y + 2, 0), w], pairsem(s_fw, 0, b))
        landed(amp.at[b, halfspot(y + 2, 1), w], pairsem(s_fw, 1, b))
        part = rows(base, 384)
        send(amp.at[b, part, w], amp.at[b, part, w], pairsem(s_sib, b), sibling)

    def cols(k):
        return slice(k * 256, k * 256 + 256)

    def plain(b, s):
        return lambda k: jnp.dot(amp[b, cols(k), :], slab[s], preferred_element_type=F32)

    def turned(b, s):
        return lambda k: lax.dot_general(
            amp[b, :, cols(k)], slab[s], (((0,), (0,)), ((), ())), preferred_element_type=F32)

    def diagonal(b):
        def term(k):
            if k == 0:
                return lax.dot_general(
                    amp[b, :, 0:256], slab[b], (((0,), (0,)), ((), ())), preferred_element_type=F32)
            low = jnp.dot(amp[b, cols(k), 0:256], slab[b, 0:256, :], preferred_element_type=F32)
            mid = jnp.dot(amp[b, cols(k - 1), 256:512], slab[b, 256:512, :], preferred_element_type=F32)
            if k == 1:
                high = lax.dot_general(
                    amp[b, 256:512, 256:512], slab[b, 512:768, :], (((0,), (0,)), ((), ())),
                    preferred_element_type=F32)
            else:
                high = jnp.dot(amp[b, 512:768, 256:512], slab[b, 512:768, :], preferred_element_type=F32)
            return low + mid + high
        return term

    def turned_unit(j, s):
        return lambda k: lax.dot_general(
            amp[3 + k, :, cols(j)], slab[s], (((0,), (0,)), ((), ())), preferred_element_type=F32)

    def units(j, s):
        def term(k):
            value = None
            for i in range(3):
                part = jnp.dot(amp[3 + i, cols(k), cols(j)], slab[s, cols(i), :], preferred_element_type=F32)
                value = part if value is None else value + part
            return value
        return term

    def total_of(terms, k):
        value = terms[0](k)
        for term in terms[1:]:
            value = value + term(k)
        return value

    def accumulate_one(which, terms, first, k):
        value = total_of(terms, k)
        gam[which, cols(k), :] = value if first else gam[which, cols(k), :] + value

    def accumulate(which, terms, first):
        for k in range(3):
            accumulate_one(which, terms, first, k)

    def hand_back(k):
        bsend[0, cols(k), :] = total_of(
            [turned_unit(0, 0), turned_unit(1, 1), turned(6, 4)], k).astype(BF16)
        send(bsend.at[0, cols(k)], back.at[cols(k), mine],
             (s_back.at[0, 0, k], s_back.at[1, core, k]), (dn2 + 1, a))
        bsend[1, cols(k), :] = total_of([turned_unit(2, 0), plain(6, 2)], k).astype(BF16)
        send(bsend.at[1, cols(k)], back.at[cols(k), mine],
             (s_back.at[0, 1, k], s_back.at[1, core, k]), (up2, a))

    def stage_z(b):
        landed(amp.at[b, rows(384 - base, 384), wide(b)], pairsem(s_sib, b))

    def stage_a(which):
        accumulate(which, [plain(2, 0), diagonal(1)] if which else [diagonal(0), turned(2, 1)], True)

    def stage_c(which):
        accumulate(which, [units(1, 2)] if which else [units(0, 2), units(2, 4)], False)

    def keep(which, k):
        return pltpu.make_async_copy(gam.at[which, cols(k)], out.at[cols(k), mine], s_out.at[2, k])

    def hand_over(which, k):
        return remote(gam.at[which, cols(k)], out.at[cols(k), mine], pairsem(s_out, k), sibling)

    def stage_d(b):
        which = 1 if b == 7 else 0
        for k in range(3):
            need(5 if b == 8 else 3, k)
        for k in range(3):
            accumulate_one(which, [plain(7, 3) if b == 7 else turned(8, 5)], False, k)

            @pl.when(core == which)
            def _():
                keep(which, k).start()

            @pl.when(core != which)
            def _():
                hand_over(which, k).start()

    stages = dict(P=stage_p, Q=stage_q, R=stage_r, T=stage_t, U=stage_u, W=stage_w, Y=stage_y, Z=stage_z,
                  N=stage_n, B=hand_back, A=stage_a, C=stage_c, D=stage_d)
    for stage, b in ORDER:
        stages[stage](b)
    for k in range(3):
        landed(out.at[cols(k), other], pairsem(s_out, k))
        for j in range(2):
            landed(back.at[cols(k), j * 768:j * 768 + 768], (s_back.at[0, 0, k], s_back.at[1, j, k]))
        for which in range(2):
            @pl.when(core == which)
            def _():
                keep(which, k).wait()

            @pl.when(core != which)
            def _():
                hand_over(which, k).wait_send()
    for i in range(12 - AHEAD, 12):
        for d in range(2):
            chunks[d, i].wait_send()
    for copy in pending + list(gives.values()):
        copy.wait_send()


def per_device(orbital_b, block_size, occ_energy, virt_energy):
    block = orbital_b.reshape(768, 1536)
    dma = pltpu.SemaphoreType.DMA
    vmem = pltpu.VMEM
    partial, shares = pl.pallas_call(
        kernel,
        out_shape=(jax.ShapeDtypeStruct((768, 1536), F32), jax.ShapeDtypeStruct((768, 1536), BF16)),
        in_specs=[
            pl.BlockSpec(memory_space=pl.ANY),
            pl.BlockSpec(memory_space=pltpu.SMEM),
            pl.BlockSpec(memory_space=pltpu.SMEM),
            pl.BlockSpec(memory_space=pltpu.VMEM),
        ],
        out_specs=(pl.BlockSpec(memory_space=pl.ANY), pl.BlockSpec(memory_space=pl.ANY)),
        scratch_shapes=[
            vmem((768, 1536), BF16),
            vmem((768, 768), BF16),
            vmem((6, 768, 768), BF16),
            vmem((3, 384, 768), F32),
            vmem((3, 384, 768), F32),
            vmem((N_PAIR, 384, 768), F32),
            vmem((N_PAIR, 96, 768), BF16),
            vmem((2, N_PAIR, 48, 768), BF16),
            vmem((2, N_PAIR, 96, 768), BF16),
            vmem((2, N_PAIR, 96, 768), BF16),
            vmem((N_PAIR, 96, 768), BF16),
            vmem((N_PAIR, 96, 768), BF16),
            vmem((N_PAIR + 1, 768, 768), BF16),
            vmem((2, 768, 768), F32),
            vmem((2, 768, 768), BF16),
            vmem((512, 128), F32),
            dma((2, 2)),
            dma((2, 2, 12)),
            dma((2, N_PAIR)),
            dma((2, 2, N_PAIR)),
            dma((2, 2, N_PAIR)),
            dma((2, N_PAIR)),
            dma((2, 2, N_PAIR + 1)),
            dma((2, 2, N_PAIR + 1)),
            dma((2, N_PAIR + 1)),
            dma((2,)),
            dma((2, 2, 3)),
            dma((3, 3)),
            dma,
        ],
        compiler_params=pltpu.CompilerParams(
            collective_id=0, has_side_effects=True, vmem_limit_bytes=62 * 2**20),
        name="window_gamma",
    )(block, block_size, occ_energy, virt_energy.reshape(1, 256))
    return (partial + shares.astype(F32)).reshape(3, 256, 1536)


def solution(mesh):
    in_specs = (P("occ", None, "aux"), P(), P(), P())
    out_specs = P("occ", None, "aux")
    return jax.shard_map(
        per_device, mesh=mesh, in_specs=in_specs, out_specs=out_specs, check_vma=False
    )
```

```python
import jax
import jax.numpy as jnp
from jax import lax
from jax.experimental import pallas as pl
from jax.experimental.pallas import tpu as pltpu
from jax.sharding import PartitionSpec as P

MESH = pl.DeviceIdType.MESH
BF16 = jnp.bfloat16
F32 = jnp.float32

SLAB_SHIFT = (0, 1, -1, -2, 2, 3)
PACKED = 3
BATCHES = (
    ((0, 0, 0), (0, 0, PACKED)),
    ((1, 1, 0), (1, 1, PACKED)),
    tuple((1, 0, k) for k in range(3)),
    ((0, 2, 0), (1, 2, 0), (0, 4, 0)),
    ((0, 2, 1), (1, 2, 1), (0, 4, 1)),
    ((0, 2, 2), (1, 2, 2), (0, 4, 2)),
    tuple((4, 2, k) for k in range(3)),
    tuple((1, 3, k) for k in range(3)),
)
N_PAIR = len(BATCHES)
AHEAD = 2

ORDER = (
    ("P", 0), ("P", 2), ("P", 1), ("Q", 0), ("Q", 2), ("N", 0), ("Q", 1), ("R", 2), ("N", 1), ("P", 3),
    ("N", 2), ("Q", 3), ("R", 3), ("R", 0), ("N", 3), ("P", 4), ("N", 4), ("T", 3), ("Q", 4), ("R", 1),
    ("R", 4), ("N", 5), ("T", 0), ("P", 5), ("P", 6), ("N", 6), ("Q", 6), ("R", 6), ("U", 3), ("N", 7),
    ("Q", 5), ("U", 0), ("T", 6), ("N", 8), ("W", 3), ("R", 5), ("T", 2), ("N", 9), ("W", 0), ("Y", 3),
    ("Z", 3), ("U", 6), ("T", 5), ("T", 4), ("T", 1), ("Y", 0), ("Z", 0), ("W", 6), ("U", 2), ("P", 7),
    ("Y", 6), ("Q", 7), ("Z", 6), ("U", 5), ("B", 0), ("R", 7), ("U", 4), ("U", 1), ("W", 5), ("T", 7),
    ("W", 4), ("W", 2), ("W", 1), ("Y", 5), ("U", 7), ("Z", 5), ("Y", 4), ("B", 2), ("Y", 2), ("Z", 4),
    ("B", 1), ("Y", 1), ("Z", 2), ("U", 8), ("W", 7), ("Z", 1), ("A", 1), ("A", 0), ("W", 8), ("C", 0),
    ("Y", 7), ("C", 1), ("Y", 8), ("Z", 7), ("D", 7), ("Z", 8), ("D", 8),
)


def rows(start, size, align=16):
    return pl.ds(pl.multiple_of(start, align), size)


def kernel(orb_hbm, sizes, occ_e, virt, out, back, orb, swap, slab, own, give, half, c1, d1, c2, e2, f1, f2,
           amp, gam, bsend, vcol, s_swap, s_slab, s_half, s_c1, s_c2, s_f, s_ay, s_fw,
           s_sib, s_z8, s_back, s_out, s_load):
    o = lax.axis_index("occ")
    a = lax.axis_index("aux")
    chip, core = o // 2, o % 2
    xh, y = a // 4, a % 4
    sibling = (chip * 2 + 1 - core, a)
    up2 = ((chip + 1) % 8) * 2
    dn2 = ((chip + 7) % 8) * 2
    below = (dn2 + core, a)
    yup = (o, xh * 4 + (y + 1) % 4)
    ydn = (o, xh * 4 + (y + 3) % 4)
    xpart = (o, (1 - xh) * 4 + y)
    partners = (sibling, yup, ydn, xpart, (up2, a), (up2 + 1, a), (dn2, a), (dn2 + 1, a))

    load = pltpu.make_async_copy(orb_hbm, orb, s_load)
    load.start()
    barrier = pltpu.get_barrier_semaphore()
    for device in partners:
        pl.semaphore_signal(barrier, inc=1, device_id=device, device_id_type=MESH)
    pending = []

    def remote(src, dst, sems, device):
        copy = pltpu.make_async_remote_copy(
            src_ref=src, dst_ref=dst, send_sem=sems[0], recv_sem=sems[1], device_id=device,
            device_id_type=MESH)
        return copy

    def send(src, dst, sems, device):
        copy = remote(src, dst, sems, device)
        copy.start()
        pending.append(copy)
        return copy

    def landed(dst, sems):
        remote(dst, dst, sems, sibling).wait_recv()

    def pairsem(sem, *index):
        return sem.at[(0,) + index], sem.at[(1,) + index]

    mine = pl.ds(pl.multiple_of(core * 768, 128), 768)
    other = pl.ds(pl.multiple_of((1 - core) * 768, 128), 768)
    live = sizes[o]

    def mask_other(i, _):
        r = rows(i * 64, 64)
        swap[r, :] = jnp.where(i // 4 < live, orb[r, other], jnp.zeros((64, 768), BF16))
        return 0

    def mask_mine(i, _):
        r = rows(i * 64, 64)
        slab[core, r, :] = jnp.where(i // 4 < live, orb[r, mine], jnp.zeros((64, 768), BF16))
        return 0

    load.wait()
    lax.fori_loop(0, 12, mask_mine, 0)
    pl.semaphore_wait(barrier, len(partners))

    def chunk_copy(d, i):
        part = slice(i % 6 * 128, i % 6 * 128 + 128)
        which, index, chip2 = (1 - i // 6, 2 + i // 6, up2) if d == 0 else (i // 6, 4 + i // 6, dn2)
        return remote(slab.at[which, part], slab.at[index, part], pairsem(s_slab, d, i), (chip2 + core, a))

    def first_chunk(which, i):
        part = slice(i * 128, i * 128 + 128)
        chip2 = up2 * which + dn2 * (1 - which)
        remote(slab.at[which, part], slab.at[4 - 2 * which, part], pairsem(s_slab, 1 - which, i),
               (chip2 + core, a)).start()

    chunks = {}
    for i in range(AHEAD):
        first_chunk(core, i)
    lax.fori_loop(0, 12, mask_other, 0)
    send(swap.at[0:256], slab.at[core, 0:256], pairsem(s_swap, 0), sibling)
    send(swap.at[256:768], slab.at[core, 256:768], pairsem(s_swap, 1), sibling)
    landed(slab.at[1 - core, 0:256], pairsem(s_swap, 0))
    for i in range(AHEAD):
        first_chunk(1 - core, i)
        for d in range(2):
            chunks[d, i] = chunk_copy(d, i)

    column = jnp.broadcast_to(virt[...], (128, 256)).T
    vcol[0:256, :] = column
    vcol[256:512, :] = column

    landed(slab.at[1 - core, 256:768], pairsem(s_swap, 1))
    arrived = set()

    def need(index, k):
        if index < 2 or (index, k) in arrived:
            return
        d, late = (index - 2) // 2, index % 2 * 6
        for i in (2 * k, 2 * k + 1):
            landed(slab.at[index, i * 128:i * 128 + 128], pairsem(s_slab, d, late + i))
        arrived.add((index, k))

    def stage_n(i):
        for d in range(2):
            chunks[d, i].wait_send()
            chunks[d, i + AHEAD] = chunk_copy(d, i + AHEAD)
            chunks[d, i + AHEAD].start()

    base = core * 384
    r_own = y * 96
    r_up = ((y + 1) % 4) * 96
    r_dn = ((y + 3) % 4) * 96
    r_far = ((y + 2) % 4) * 96
    gives, taken = {}, {}

    def stage_p(b):
        for left, right, k in BATCHES[b]:
            need(right, k)
            for i in range(3):
                need(left, i)
        slot = taken[b] = min({0, 1, 2} - set(taken.values()))
        if slot in gives:
            gives[slot].wait_send()

        def product(dst, side):
            for j, (left, right, k) in enumerate(BATCHES[b]):
                lanes = slice(j * 256, j * 256 + 256)
                if k == PACKED:
                    for p in range(3):
                        row = 256 + 128 * p + side * (384, 128, 128)[p]
                        col = 256 + side * (0, 256, 256)[p]
                        dst[slot, p * 128:p * 128 + 128, lanes] = lax.dot_general(
                            slab[left, rows(row, 128), :], slab[right, rows(col, 256), :],
                            (((1,), (1,)), ((), ())), preferred_element_type=F32)
                else:
                    dst[slot, :, lanes] = lax.dot_general(
                        slab[left, rows(side * 384, 384), :], slab[right, k * 256:k * 256 + 256, :],
                        (((1,), (1,)), ((), ())), preferred_element_type=F32)

        w = wide(b)
        product(give, 1 - core)
        gives[slot] = remote(give.at[slot, :, w], half.at[b, :, w], pairsem(s_half, b), sibling)
        gives[slot].start()
        product(own, core)

    def wide(b):
        return slice(0, 256 * len(BATCHES[min(b, 7)]))

    def stage_q(b):
        slot, w = taken.pop(b), wide(b)
        landed(half.at[b, :, w], pairsem(s_half, b))

        def far(i, _):
            r = rows(r_far + i * 48, 48)
            c1[b, rows(i * 48, 48), w] = (half[b, r, w] + own[slot, r, w]).astype(BF16)
            return 0

        lax.fori_loop(0, 2, far, 0)
        send(c1.at[b, 0:48, w], d1.at[0, b, :, w], pairsem(s_c1, 0, b), yup)
        send(c1.at[b, 48:96, w], d1.at[1, b, :, w], pairsem(s_c1, 1, b), ydn)

        def add(i, _):
            r = rows(i * 48, 48)
            half[b, r, w] = half[b, r, w] + own[slot, r, w]
            return 0

        lax.fori_loop(0, 8, add, 0)

    def stage_r(b):
        w = wide(b)
        landed(d1.at[0, b, :, w], pairsem(s_c1, 0, b))
        c2[0, b, 0:48, w] = (half[b, rows(r_up, 48), w] + d1[0, b, :, w].astype(F32)).astype(BF16)
        c2[0, b, 48:96, w] = half[b, rows(r_up + 48, 48), w].astype(BF16)
        send(c2.at[0, b, :, w], e2.at[0, b, :, w], pairsem(s_c2, 0, b), yup)
        landed(d1.at[1, b, :, w], pairsem(s_c1, 1, b))
        c2[1, b, 0:48, w] = half[b, rows(r_dn, 48), w].astype(BF16)
        c2[1, b, 48:96, w] = (half[b, rows(r_dn + 48, 48), w] + d1[1, b, :, w].astype(F32)).astype(BF16)
        send(c2.at[1, b, :, w], e2.at[1, b, :, w], pairsem(s_c2, 1, b), ydn)

    def stage_t(b):
        w = wide(b)
        landed(e2.at[0, b, :, w], pairsem(s_c2, 0, b))
        landed(e2.at[1, b, :, w], pairsem(s_c2, 1, b))

        def total(i, _):
            r = rows(r_own + i * 48, 48)
            q = rows(i * 48, 48)
            value = half[b, r, w] + (e2[0, b, q, w].astype(F32) + e2[1, b, q, w].astype(F32))
            half[b, r, w] = value
            f1[b, q, w] = value.astype(BF16)
            return 0

        lax.fori_loop(0, 2, total, 0)
        send(f1.at[b, :, w], f2.at[b, :, w], pairsem(s_f, b), xpart)

    def block(index):
        return (chip * 2 + SLAB_SHIFT[index] + 16) % 16

    def spot(yy):
        return rows(base + ((yy + 4) % 4) * 96, 96)

    def halfspot(yy, i):
        return rows(base + ((yy + 4) % 4) * 96 + i * 48, 48)

    def send_spot(b, where, sem, device):
        send(amp.at[b, where, wide(b)], amp.at[b, where, wide(b)], sem, device)

    def stage_u(b):
        here = spot(y)
        if b < N_PAIR:
            landed(f2.at[b, :, wide(b)], pairsem(s_f, b))
            first = base + r_own
            within = first % 256
            group = first // 256
            after = jnp.minimum(group + 1, 2)
            step = lax.broadcasted_iota(jnp.int32, (96, 256), 0) + within
            down = vcol[rows(within, 96), :]
            down = jnp.concatenate([down, down], axis=1)
            for j, (left, right, k) in enumerate(BATCHES[b]):
                def energy(which, slots):
                    first_e = occ_e[block(which) * 3 + slots[0]]
                    return jnp.where(step < 256, first_e, occ_e[block(which) * 3 + slots[1]])
                if k == PACKED:
                    row_e = down - energy(left, (jnp.minimum(group + 1, 2), jnp.minimum(after + 1, 2)))
                    col_e = virt[...] - energy(right, (1 + group // 2, 1 + after // 2))
                else:
                    row_e = down - energy(left, (group, after))
                    col_e = virt[...] - occ_e[block(right) * 3 + k]
                lanes = slice(j * 256, j * 256 + 256)
                value = half[b, rows(r_own, 96), lanes] + f2[b, :, lanes].astype(F32)
                amp[b, here, lanes] = (value / (row_e + col_e)).astype(BF16)
            if b == 7:
                send(amp.at[7, here], amp.at[8, here], pairsem(s_z8), below)
        else:
            landed(amp.at[8, here], pairsem(s_z8))
        send_spot(b, here, pairsem(s_ay, 0, b), yup)
        send_spot(b, here, pairsem(s_ay, 1, b), ydn)

    def stage_w(b):
        w = wide(b)
        landed(amp.at[b, spot(y - 1), w], pairsem(s_ay, 0, b))
        send_spot(b, halfspot(y - 1, 0), pairsem(s_fw, 0, b), yup)
        landed(amp.at[b, spot(y + 1), w], pairsem(s_ay, 1, b))
        send_spot(b, halfspot(y + 1, 1), pairsem(s_fw, 1, b), ydn)

    def stage_y(b):
        w = wide(b)
        landed(amp.at[b, halfspot(y + 2, 0), w], pairsem(s_fw, 0, b))
        landed(amp.at[b, halfspot(y + 2, 1), w], pairsem(s_fw, 1, b))
        part = rows(base, 384)
        send(amp.at[b, part, w], amp.at[b, part, w], pairsem(s_sib, b), sibling)

    def cols(k):
        return slice(k * 256, k * 256 + 256)

    def plain(b, s):
        return lambda k: jnp.dot(amp[b, cols(k), :], slab[s], preferred_element_type=F32)

    def turned(b, s):
        return lambda k: lax.dot_general(
            amp[b, :, cols(k)], slab[s], (((0,), (0,)), ((), ())), preferred_element_type=F32)

    def diagonal(b):
        def term(k):
            if k == 0:
                return lax.dot_general(
                    amp[b, :, 0:256], slab[b], (((0,), (0,)), ((), ())), preferred_element_type=F32)
            low = jnp.dot(amp[b, cols(k), 0:256], slab[b, 0:256, :], preferred_element_type=F32)
            mid = jnp.dot(amp[b, cols(k - 1), 256:512], slab[b, 256:512, :], preferred_element_type=F32)
            if k == 1:
                high = lax.dot_general(
                    amp[b, 256:512, 256:512], slab[b, 512:768, :], (((0,), (0,)), ((), ())),
                    preferred_element_type=F32)
            else:
                high = jnp.dot(amp[b, 512:768, 256:512], slab[b, 512:768, :], preferred_element_type=F32)
            return low + mid + high
        return term

    def turned_unit(j, s):
        return lambda k: lax.dot_general(
            amp[3 + k, :, cols(j)], slab[s], (((0,), (0,)), ((), ())), preferred_element_type=F32)

    def units(j, s):
        def term(k):
            value = None
            for i in range(3):
                part = jnp.dot(amp[3 + i, cols(k), cols(j)], slab[s, cols(i), :], preferred_element_type=F32)
                value = part if value is None else value + part
            return value
        return term

    def total_of(terms, k):
        value = terms[0](k)
        for term in terms[1:]:
            value = value + term(k)
        return value

    def accumulate_one(which, terms, first, k):
        value = total_of(terms, k)
        gam[which, cols(k), :] = value if first else gam[which, cols(k), :] + value

    def accumulate(which, terms, first):
        for k in range(3):
            accumulate_one(which, terms, first, k)

    def hand_back(k):
        bsend[0, cols(k), :] = total_of(
            [turned_unit(0, 0), turned_unit(1, 1), turned(6, 4)], k).astype(BF16)
        send(bsend.at[0, cols(k)], back.at[cols(k), mine],
             (s_back.at[0, 0, k], s_back.at[1, core, k]), (dn2 + 1, a))
        bsend[1, cols(k), :] = total_of([turned_unit(2, 0), plain(6, 2)], k).astype(BF16)
        send(bsend.at[1, cols(k)], back.at[cols(k), mine],
             (s_back.at[0, 1, k], s_back.at[1, core, k]), (up2, a))

    def stage_z(b):
        landed(amp.at[b, rows(384 - base, 384), wide(b)], pairsem(s_sib, b))

    def stage_a(which):
        accumulate(which, [plain(2, 0), diagonal(1)] if which else [diagonal(0), turned(2, 1)], True)

    def stage_c(which):
        accumulate(which, [units(1, 2)] if which else [units(0, 2), units(2, 4)], False)

    def keep(which, k):
        return pltpu.make_async_copy(gam.at[which, cols(k)], out.at[cols(k), mine], s_out.at[2, k])

    def hand_over(which, k):
        return remote(gam.at[which, cols(k)], out.at[cols(k), mine], pairsem(s_out, k), sibling)

    def stage_d(b):
        which = 1 if b == 7 else 0
        for k in range(3):
            need(5 if b == 8 else 3, k)
        for k in range(3):
            accumulate_one(which, [plain(7, 3) if b == 7 else turned(8, 5)], False, k)

            @pl.when(core == which)
            def _():
                keep(which, k).start()

            @pl.when(core != which)
            def _():
                hand_over(which, k).start()

    stages = dict(P=stage_p, Q=stage_q, R=stage_r, T=stage_t, U=stage_u, W=stage_w, Y=stage_y, Z=stage_z,
                  N=stage_n, B=hand_back, A=stage_a, C=stage_c, D=stage_d)
    for stage, b in ORDER:
        stages[stage](b)
    for k in range(3):
        landed(out.at[cols(k), other], pairsem(s_out, k))
        for j in range(2):
            landed(back.at[cols(k), j * 768:j * 768 + 768], (s_back.at[0, 0, k], s_back.at[1, j, k]))
        for which in range(2):
            @pl.when(core == which)
            def _():
                keep(which, k).wait()

            @pl.when(core != which)
            def _():
                hand_over(which, k).wait_send()
    for i in range(12 - AHEAD, 12):
        for d in range(2):
            chunks[d, i].wait_send()
    for copy in pending + list(gives.values()):
        copy.wait_send()


def add_shares(partial, shares, out):
    out[...] = partial[...] + shares[...].astype(F32)


def per_device(orbital_b, block_size, occ_energy, virt_energy):
    block = orbital_b.reshape(768, 1536)
    dma = pltpu.SemaphoreType.DMA
    vmem = pltpu.VMEM
    partial, shares = pl.pallas_call(
        kernel,
        out_shape=(jax.ShapeDtypeStruct((768, 1536), F32), jax.ShapeDtypeStruct((768, 1536), BF16)),
        in_specs=[
            pl.BlockSpec(memory_space=pl.ANY),
            pl.BlockSpec(memory_space=pltpu.SMEM),
            pl.BlockSpec(memory_space=pltpu.SMEM),
            pl.BlockSpec(memory_space=pltpu.VMEM),
        ],
        out_specs=(pl.BlockSpec(memory_space=pl.ANY), pl.BlockSpec(memory_space=pl.ANY)),
        scratch_shapes=[
            vmem((768, 1536), BF16),
            vmem((768, 768), BF16),
            vmem((6, 768, 768), BF16),
            vmem((3, 384, 768), F32),
            vmem((3, 384, 768), F32),
            vmem((N_PAIR, 384, 768), F32),
            vmem((N_PAIR, 96, 768), BF16),
            vmem((2, N_PAIR, 48, 768), BF16),
            vmem((2, N_PAIR, 96, 768), BF16),
            vmem((2, N_PAIR, 96, 768), BF16),
            vmem((N_PAIR, 96, 768), BF16),
            vmem((N_PAIR, 96, 768), BF16),
            vmem((N_PAIR + 1, 768, 768), BF16),
            vmem((2, 768, 768), F32),
            vmem((2, 768, 768), BF16),
            vmem((512, 128), F32),
            dma((2, 2)),
            dma((2, 2, 12)),
            dma((2, N_PAIR)),
            dma((2, 2, N_PAIR)),
            dma((2, 2, N_PAIR)),
            dma((2, N_PAIR)),
            dma((2, 2, N_PAIR + 1)),
            dma((2, 2, N_PAIR + 1)),
            dma((2, N_PAIR + 1)),
            dma((2,)),
            dma((2, 2, 3)),
            dma((3, 3)),
            dma,
        ],
        compiler_params=pltpu.CompilerParams(
            collective_id=0, has_side_effects=True, vmem_limit_bytes=62 * 2**20),
        name="window_gamma",
    )(block, block_size, occ_energy, virt_energy.reshape(1, 256))
    step = pl.BlockSpec((96, 1536), lambda i: (i, 0))
    total = pl.pallas_call(
        add_shares,
        out_shape=jax.ShapeDtypeStruct((768, 1536), F32),
        grid=(8,),
        in_specs=[step, step],
        out_specs=step,
        compiler_params=pltpu.CompilerParams(vmem_limit_bytes=62 * 2**20),
        name="add_shares",
    )(partial, shares)
    return total.reshape(3, 256, 1536)


def solution(mesh):
    in_specs = (P("occ", None, "aux"), P(), P(), P())
    out_specs = P("occ", None, "aux")
    return jax.shard_map(
        per_device, mesh=mesh, in_specs=in_specs, out_specs=out_specs, check_vma=False
    )
```

```python
import jax
import jax.numpy as jnp
from jax import lax
from jax.experimental import pallas as pl
from jax.experimental.pallas import tpu as pltpu
from jax.sharding import PartitionSpec as P

MESH = pl.DeviceIdType.MESH
BF16 = jnp.bfloat16
F32 = jnp.float32

SLAB_SHIFT = (0, 1, -1, -2, 2, 3)
PACKED = 3
BATCHES = (
    ((0, 0, 0), (0, 0, PACKED)),
    ((1, 1, 0), (1, 1, PACKED)),
    tuple((1, 0, k) for k in range(3)),
    ((0, 2, 0), (1, 2, 0), (0, 4, 0)),
    ((0, 2, 1), (1, 2, 1), (0, 4, 1)),
    ((0, 2, 2), (1, 2, 2), (0, 4, 2)),
    tuple((4, 2, k) for k in range(3)),
    tuple((1, 3, k) for k in range(3)),
)
N_PAIR = len(BATCHES)
AHEAD = 2

ORDER = (
    ("P", 0), ("P", 2), ("P", 1), ("Q", 0), ("Q", 2), ("N", 0), ("Q", 1), ("R", 2), ("N", 1), ("P", 3),
    ("N", 2), ("Q", 3), ("R", 3), ("R", 0), ("N", 3), ("P", 4), ("N", 4), ("T", 3), ("Q", 4), ("R", 1),
    ("R", 4), ("N", 5), ("T", 0), ("P", 5), ("P", 6), ("N", 6), ("Q", 6), ("R", 6), ("U", 3), ("N", 7),
    ("Q", 5), ("U", 0), ("T", 6), ("N", 8), ("W", 3), ("R", 5), ("T", 2), ("N", 9), ("W", 0), ("Y", 3),
    ("Z", 3), ("U", 6), ("T", 5), ("T", 4), ("T", 1), ("Y", 0), ("Z", 0), ("W", 6), ("U", 2), ("P", 7),
    ("Y", 6), ("Q", 7), ("Z", 6), ("U", 5), ("B", 0), ("R", 7), ("U", 4), ("U", 1), ("W", 5), ("T", 7),
    ("W", 4), ("W", 2), ("W", 1), ("Y", 5), ("U", 7), ("Z", 5), ("Y", 4), ("B", 2), ("Y", 2), ("Z", 4),
    ("B", 1), ("Y", 1), ("Z", 2), ("U", 8), ("W", 7), ("Z", 1), ("A", 1), ("A", 0), ("W", 8), ("C", 0),
    ("Y", 7), ("C", 1), ("Y", 8), ("Z", 7), ("D", 7), ("Z", 8), ("D", 8),
)


def rows(start, size, align=16):
    return pl.ds(pl.multiple_of(start, align), size)


def kernel(orb_hbm, sizes, occ_e, virt, out, back, orb, swap, slab, own, give, half, c1, d1, c2, e2, f1, f2,
           amp, gam, bsend, vcol, s_swap, s_slab, s_half, s_c1, s_c2, s_f, s_ay, s_fw,
           s_sib, s_z8, s_back, s_out, s_load):
    o = lax.axis_index("occ")
    a = lax.axis_index("aux")
    chip, core = o // 2, o % 2
    xh, y = a // 4, a % 4
    sibling = (chip * 2 + 1 - core, a)
    up2 = ((chip + 1) % 8) * 2
    dn2 = ((chip + 7) % 8) * 2
    below = (dn2 + core, a)
    yup = (o, xh * 4 + (y + 1) % 4)
    ydn = (o, xh * 4 + (y + 3) % 4)
    xpart = (o, (1 - xh) * 4 + y)
    partners = (sibling, yup, ydn, xpart, (up2, a), (up2 + 1, a), (dn2, a), (dn2 + 1, a))

    load = pltpu.make_async_copy(orb_hbm, orb, s_load)
    load.start()
    barrier = pltpu.get_barrier_semaphore()
    for device in partners:
        pl.semaphore_signal(barrier, inc=1, device_id=device, device_id_type=MESH)
    pending = []

    def remote(src, dst, sems, device):
        copy = pltpu.make_async_remote_copy(
            src_ref=src, dst_ref=dst, send_sem=sems[0], recv_sem=sems[1], device_id=device,
            device_id_type=MESH)
        return copy

    def send(src, dst, sems, device):
        copy = remote(src, dst, sems, device)
        copy.start()
        pending.append(copy)
        return copy

    def landed(dst, sems):
        remote(dst, dst, sems, sibling).wait_recv()

    def pairsem(sem, *index):
        return sem.at[(0,) + index], sem.at[(1,) + index]

    mine = pl.ds(pl.multiple_of(core * 768, 128), 768)
    other = pl.ds(pl.multiple_of((1 - core) * 768, 128), 768)
    live = sizes[o]

    def mask_other(i, _):
        r = rows(i * 64, 64)
        swap[r, :] = jnp.where(i // 4 < live, orb[r, other], jnp.zeros((64, 768), BF16))
        return 0

    def mask_mine(i, _):
        r = rows(i * 64, 64)
        slab[core, r, :] = jnp.where(i // 4 < live, orb[r, mine], jnp.zeros((64, 768), BF16))
        return 0

    load.wait()
    lax.fori_loop(0, 12, mask_mine, 0)
    pl.semaphore_wait(barrier, len(partners))

    def chunk_copy(d, i):
        part = slice(i % 6 * 128, i % 6 * 128 + 128)
        which, index, chip2 = (1 - i // 6, 2 + i // 6, up2) if d == 0 else (i // 6, 4 + i // 6, dn2)
        return remote(slab.at[which, part], slab.at[index, part], pairsem(s_slab, d, i), (chip2 + core, a))

    def first_chunk(which, i):
        part = slice(i * 128, i * 128 + 128)
        chip2 = up2 * which + dn2 * (1 - which)
        remote(slab.at[which, part], slab.at[4 - 2 * which, part], pairsem(s_slab, 1 - which, i),
               (chip2 + core, a)).start()

    chunks = {}
    for i in range(AHEAD):
        first_chunk(core, i)
    lax.fori_loop(0, 12, mask_other, 0)
    send(swap.at[0:256], slab.at[core, 0:256], pairsem(s_swap, 0), sibling)
    send(swap.at[256:768], slab.at[core, 256:768], pairsem(s_swap, 1), sibling)
    landed(slab.at[1 - core, 0:256], pairsem(s_swap, 0))
    for i in range(AHEAD):
        first_chunk(1 - core, i)
        for d in range(2):
            chunks[d, i] = chunk_copy(d, i)

    column = jnp.broadcast_to(virt[...], (128, 256)).T
    vcol[0:256, :] = column
    vcol[256:512, :] = column

    landed(slab.at[1 - core, 256:768], pairsem(s_swap, 1))
    arrived = set()

    def need(index, k):
        if index < 2 or (index, k) in arrived:
            return
        d, late = (index - 2) // 2, index % 2 * 6
        for i in (2 * k, 2 * k + 1):
            landed(slab.at[index, i * 128:i * 128 + 128], pairsem(s_slab, d, late + i))
        arrived.add((index, k))

    def stage_n(i):
        for d in range(2):
            chunks[d, i].wait_send()
            chunks[d, i + AHEAD] = chunk_copy(d, i + AHEAD)
            chunks[d, i + AHEAD].start()

    base = core * 384
    r_own = y * 96
    r_up = ((y + 1) % 4) * 96
    r_dn = ((y + 3) % 4) * 96
    r_far = ((y + 2) % 4) * 96
    gives, taken = {}, {}

    def stage_p(b):
        for left, right, k in BATCHES[b]:
            need(right, k)
            for i in range(3):
                need(left, i)
        slot = taken[b] = min({0, 1, 2} - set(taken.values()))
        if slot in gives:
            gives[slot].wait_send()

        def product(dst, side):
            for j, (left, right, k) in enumerate(BATCHES[b]):
                lanes = slice(j * 256, j * 256 + 256)
                if k == PACKED:
                    for p in range(3):
                        row = 256 + 128 * p + side * (384, 128, 128)[p]
                        col = 256 + side * (0, 256, 256)[p]
                        dst[slot, p * 128:p * 128 + 128, lanes] = lax.dot_general(
                            slab[left, rows(row, 128), :], slab[right, rows(col, 256), :],
                            (((1,), (1,)), ((), ())), preferred_element_type=F32)
                else:
                    dst[slot, :, lanes] = lax.dot_general(
                        slab[left, rows(side * 384, 384), :], slab[right, k * 256:k * 256 + 256, :],
                        (((1,), (1,)), ((), ())), preferred_element_type=F32)

        w = wide(b)
        product(give, 1 - core)
        gives[slot] = remote(give.at[slot, :, w], half.at[b, :, w], pairsem(s_half, b), sibling)
        gives[slot].start()
        product(own, core)

    def wide(b):
        return slice(0, 256 * len(BATCHES[min(b, 7)]))

    def stage_q(b):
        slot, w = taken.pop(b), wide(b)
        landed(half.at[b, :, w], pairsem(s_half, b))

        def far(i, _):
            r = rows(r_far + i * 48, 48)
            c1[b, rows(i * 48, 48), w] = (half[b, r, w] + own[slot, r, w]).astype(BF16)
            return 0

        lax.fori_loop(0, 2, far, 0)
        send(c1.at[b, 0:48, w], d1.at[0, b, :, w], pairsem(s_c1, 0, b), yup)
        send(c1.at[b, 48:96, w], d1.at[1, b, :, w], pairsem(s_c1, 1, b), ydn)

        def add(i, _):
            r = rows(i * 48, 48)
            half[b, r, w] = half[b, r, w] + own[slot, r, w]
            return 0

        lax.fori_loop(0, 8, add, 0)

    def stage_r(b):
        w = wide(b)
        landed(d1.at[0, b, :, w], pairsem(s_c1, 0, b))
        c2[0, b, 0:48, w] = (half[b, rows(r_up, 48), w] + d1[0, b, :, w].astype(F32)).astype(BF16)
        c2[0, b, 48:96, w] = half[b, rows(r_up + 48, 48), w].astype(BF16)
        send(c2.at[0, b, :, w], e2.at[0, b, :, w], pairsem(s_c2, 0, b), yup)
        landed(d1.at[1, b, :, w], pairsem(s_c1, 1, b))
        c2[1, b, 0:48, w] = half[b, rows(r_dn, 48), w].astype(BF16)
        c2[1, b, 48:96, w] = (half[b, rows(r_dn + 48, 48), w] + d1[1, b, :, w].astype(F32)).astype(BF16)
        send(c2.at[1, b, :, w], e2.at[1, b, :, w], pairsem(s_c2, 1, b), ydn)

    def stage_t(b):
        w = wide(b)
        landed(e2.at[0, b, :, w], pairsem(s_c2, 0, b))
        landed(e2.at[1, b, :, w], pairsem(s_c2, 1, b))

        def total(i, _):
            r = rows(r_own + i * 48, 48)
            q = rows(i * 48, 48)
            value = half[b, r, w] + (e2[0, b, q, w].astype(F32) + e2[1, b, q, w].astype(F32))
            half[b, r, w] = value
            f1[b, q, w] = value.astype(BF16)
            return 0

        lax.fori_loop(0, 2, total, 0)
        send(f1.at[b, :, w], f2.at[b, :, w], pairsem(s_f, b), xpart)

    def block(index):
        return (chip * 2 + SLAB_SHIFT[index] + 16) % 16

    def spot(yy):
        return rows(base + ((yy + 4) % 4) * 96, 96)

    def halfspot(yy, i):
        return rows(base + ((yy + 4) % 4) * 96 + i * 48, 48)

    def send_spot(b, where, sem, device):
        send(amp.at[b, where, wide(b)], amp.at[b, where, wide(b)], sem, device)

    def stage_u(b):
        here = spot(y)
        if b < N_PAIR:
            landed(f2.at[b, :, wide(b)], pairsem(s_f, b))
            first = base + r_own
            within = first % 256
            group = first // 256
            after = jnp.minimum(group + 1, 2)
            step = lax.broadcasted_iota(jnp.int32, (96, 256), 0) + within
            down = vcol[rows(within, 96), :]
            down = jnp.concatenate([down, down], axis=1)
            for j, (left, right, k) in enumerate(BATCHES[b]):
                def energy(which, slots):
                    first_e = occ_e[block(which) * 3 + slots[0]]
                    return jnp.where(step < 256, first_e, occ_e[block(which) * 3 + slots[1]])
                if k == PACKED:
                    row_e = down - energy(left, (jnp.minimum(group + 1, 2), jnp.minimum(after + 1, 2)))
                    col_e = virt[...] - energy(right, (1 + group // 2, 1 + after // 2))
                else:
                    row_e = down - energy(left, (group, after))
                    col_e = virt[...] - occ_e[block(right) * 3 + k]
                lanes = slice(j * 256, j * 256 + 256)
                value = half[b, rows(r_own, 96), lanes] + f2[b, :, lanes].astype(F32)
                amp[b, here, lanes] = (value / (row_e + col_e)).astype(BF16)
            if b == 7:
                send(amp.at[7, here], amp.at[8, here], pairsem(s_z8), below)
        else:
            landed(amp.at[8, here], pairsem(s_z8))
        send_spot(b, here, pairsem(s_ay, 0, b), yup)
        send_spot(b, here, pairsem(s_ay, 1, b), ydn)

    def stage_w(b):
        w = wide(b)
        landed(amp.at[b, spot(y - 1), w], pairsem(s_ay, 0, b))
        send_spot(b, halfspot(y - 1, 0), pairsem(s_fw, 0, b), yup)
        landed(amp.at[b, spot(y + 1), w], pairsem(s_ay, 1, b))
        send_spot(b, halfspot(y + 1, 1), pairsem(s_fw, 1, b), ydn)

    def stage_y(b):
        w = wide(b)
        landed(amp.at[b, halfspot(y + 2, 0), w], pairsem(s_fw, 0, b))
        landed(amp.at[b, halfspot(y + 2, 1), w], pairsem(s_fw, 1, b))
        part = rows(base, 384)
        send(amp.at[b, part, w], amp.at[b, part, w], pairsem(s_sib, b), sibling)

    def cols(k):
        return slice(k * 256, k * 256 + 256)

    def plain(b, s):
        return lambda k: jnp.dot(amp[b, cols(k), :], slab[s], preferred_element_type=F32)

    def turned(b, s):
        return lambda k: lax.dot_general(
            amp[b, :, cols(k)], slab[s], (((0,), (0,)), ((), ())), preferred_element_type=F32)

    def diagonal(b):
        def term(k):
            if k == 0:
                return lax.dot_general(
                    amp[b, :, 0:256], slab[b], (((0,), (0,)), ((), ())), preferred_element_type=F32)
            low = jnp.dot(amp[b, cols(k), 0:256], slab[b, 0:256, :], preferred_element_type=F32)
            mid = jnp.dot(amp[b, cols(k - 1), 256:512], slab[b, 256:512, :], preferred_element_type=F32)
            if k == 1:
                high = lax.dot_general(
                    amp[b, 256:512, 256:512], slab[b, 512:768, :], (((0,), (0,)), ((), ())),
                    preferred_element_type=F32)
            else:
                high = jnp.dot(amp[b, 512:768, 256:512], slab[b, 512:768, :], preferred_element_type=F32)
            return low + mid + high
        return term

    def turned_unit(j, s):
        return lambda k: lax.dot_general(
            amp[3 + k, :, cols(j)], slab[s], (((0,), (0,)), ((), ())), preferred_element_type=F32)

    def units(j, s):
        def term(k):
            value = None
            for i in range(3):
                part = jnp.dot(amp[3 + i, cols(k), cols(j)], slab[s, cols(i), :], preferred_element_type=F32)
                value = part if value is None else value + part
            return value
        return term

    def total_of(terms, k):
        value = terms[0](k)
        for term in terms[1:]:
            value = value + term(k)
        return value

    def accumulate_one(which, terms, first, k):
        value = total_of(terms, k)
        gam[which, cols(k), :] = value if first else gam[which, cols(k), :] + value

    def accumulate(which, terms, first):
        for k in range(3):
            accumulate_one(which, terms, first, k)

    def hand_back(k):
        bsend[0, cols(k), :] = total_of(
            [turned_unit(0, 0), turned_unit(1, 1), turned(6, 4)], k).astype(BF16)
        send(bsend.at[0, cols(k)], back.at[cols(k), mine],
             (s_back.at[0, 0, k], s_back.at[1, core, k]), (dn2 + 1, a))
        bsend[1, cols(k), :] = total_of([turned_unit(2, 0), plain(6, 2)], k).astype(BF16)
        send(bsend.at[1, cols(k)], back.at[cols(k), mine],
             (s_back.at[0, 1, k], s_back.at[1, core, k]), (up2, a))

    def stage_z(b):
        landed(amp.at[b, rows(384 - base, 384), wide(b)], pairsem(s_sib, b))

    def stage_a(which):
        accumulate(which, [plain(2, 0), diagonal(1)] if which else [diagonal(0), turned(2, 1)], True)

    def stage_c(which):
        accumulate(which, [units(1, 2)] if which else [units(0, 2), units(2, 4)], False)

    def keep(which, k):
        return pltpu.make_async_copy(gam.at[which, cols(k)], out.at[cols(k), mine], s_out.at[2, k])

    def hand_over(which, k):
        return remote(gam.at[which, cols(k)], out.at[cols(k), mine], pairsem(s_out, k), sibling)

    def stage_d(b):
        which = 1 if b == 7 else 0
        for k in range(3):
            need(5 if b == 8 else 3, k)
        for k in range(3):
            accumulate_one(which, [plain(7, 3) if b == 7 else turned(8, 5)], False, k)

            @pl.when(core == which)
            def _():
                keep(which, k).start()

            @pl.when(core != which)
            def _():
                hand_over(which, k).start()

    stages = dict(P=stage_p, Q=stage_q, R=stage_r, T=stage_t, U=stage_u, W=stage_w, Y=stage_y, Z=stage_z,
                  N=stage_n, B=hand_back, A=stage_a, C=stage_c, D=stage_d)
    for stage, b in ORDER:
        stages[stage](b)
    for k in range(3):
        landed(out.at[cols(k), other], pairsem(s_out, k))
        for j in range(2):
            landed(back.at[cols(k), j * 768:j * 768 + 768], (s_back.at[0, 0, k], s_back.at[1, j, k]))
        for which in range(2):
            @pl.when(core == which)
            def _():
                keep(which, k).wait()

            @pl.when(core != which)
            def _():
                hand_over(which, k).wait_send()
    for i in range(12 - AHEAD, 12):
        for d in range(2):
            chunks[d, i].wait_send()
    for copy in pending + list(gives.values()):
        copy.wait_send()


def per_device(orbital_b, block_size, occ_energy, virt_energy):
    block = orbital_b.reshape(768, 1536)
    dma = pltpu.SemaphoreType.DMA
    vmem = pltpu.VMEM
    partial, shares = pl.pallas_call(
        kernel,
        out_shape=(jax.ShapeDtypeStruct((768, 1536), F32), jax.ShapeDtypeStruct((768, 1536), BF16)),
        in_specs=[
            pl.BlockSpec(memory_space=pl.ANY),
            pl.BlockSpec(memory_space=pltpu.SMEM),
            pl.BlockSpec(memory_space=pltpu.SMEM),
            pl.BlockSpec(memory_space=pltpu.VMEM),
        ],
        out_specs=(pl.BlockSpec(memory_space=pl.ANY), pl.BlockSpec(memory_space=pl.ANY)),
        scratch_shapes=[
            vmem((768, 1536), BF16),
            vmem((768, 768), BF16),
            vmem((6, 768, 768), BF16),
            vmem((3, 384, 768), F32),
            vmem((3, 384, 768), F32),
            vmem((N_PAIR, 384, 768), F32),
            vmem((N_PAIR, 96, 768), BF16),
            vmem((2, N_PAIR, 48, 768), BF16),
            vmem((2, N_PAIR, 96, 768), BF16),
            vmem((2, N_PAIR, 96, 768), BF16),
            vmem((N_PAIR, 96, 768), BF16),
            vmem((N_PAIR, 96, 768), BF16),
            vmem((N_PAIR + 1, 768, 768), BF16),
            vmem((2, 768, 768), F32),
            vmem((2, 768, 768), BF16),
            vmem((512, 128), F32),
            dma((2, 2)),
            dma((2, 2, 12)),
            dma((2, N_PAIR)),
            dma((2, 2, N_PAIR)),
            dma((2, 2, N_PAIR)),
            dma((2, N_PAIR)),
            dma((2, 2, N_PAIR + 1)),
            dma((2, 2, N_PAIR + 1)),
            dma((2, N_PAIR + 1)),
            dma((2,)),
            dma((2, 2, 3)),
            dma((3, 3)),
            dma,
        ],
        compiler_params=pltpu.CompilerParams(
            collective_id=0, has_side_effects=True, vmem_limit_bytes=62 * 2**20),
        name="window_gamma",
    )(block, block_size, occ_energy, virt_energy.reshape(1, 256))
    return (partial + shares.astype(F32)).reshape(3, 256, 1536)


def solution(mesh):
    in_specs = (P("occ", None, "aux"), P(), P(), P())
    out_specs = P("occ", None, "aux")
    return jax.shard_map(
        per_device, mesh=mesh, in_specs=in_specs, out_specs=out_specs, check_vma=False
    )
```
